32 devices in a mesh: sta: 8 (over z, y), tpl: 4 (over x, core).
Axes of the slice: x: 2, y: 2, z: 4, core: 2. Of those that a mesh axis runs over, the one named last changes fastest.
Arguments:
- window: bfloat16 [384, 1024], P('sta', 'tpl'), may hold values from -6 to 6
- prior: bfloat16 [384, 599], P('sta'), may hold values from -6 to 6
- waves: bfloat16 [32, 128, 600], P('tpl', 'sta'), may hold values from -6 to 6
- chan_list: int32 [32, 128], P('tpl', 'sta'), may hold values from 0 to 383, as said below
- chan_count: int32 [32], P('tpl'), may hold values from 21 to 120
- station_row: int32 [128], replicated, may hold values from 0 to 127, as said below
Outputs:
- stacked: float32 [32, 1024], P(('tpl', 'sta'))
The draws below stay inside these ranges and needn't reach their ends.
Inputs may be any that keep to these rules, and one draw needn't show every extreme that they name: station_row is a permutation of 0 to 127; station s's three channels are data rows 3 station_row[s] to 3 station_row[s] + 2, and its station block is station_row[s] // 16. `chan_list`: channel c is component c % 3 of station c // 3. For every group of 8 templates (g * 8 to (g + 1) * 8 - 1) and every aligned run of 16 slots, each station block is named by exactly 16 of those slots, listed or not.
All inputs are finite; a program needn't handle non-finite values.
Results may differ from the reference program's by a relative error of at most 0.0029.
Values may be sent and summed in bfloat16 or wider, within the bound.
No kernel may reach another device: no remote copies, remote signals or barrier semaphores. Data moves between devices by JAX's collectives and lax.ppermute only.
A program may use at most 64 MiB of HBM per device.

```python
import jax
import jax.numpy as jnp
from jax import lax

TLEN = 600
SLOTS = 128
STA_DEV = 16
LAGS = 1024
STATIONS = 128
CHANNELS = 384
TPL_GRP = 8
TEMPLATES = 32
SL_DEV = 16
CAP = 16
N_STA = 8
N_TPL = 4


def station_order(key):
    return jax.random.permutation(jax.random.fold_in(key, 11), STATIONS).astype(jnp.int32)


def draw_station_row(key, part):
    return station_order(key)


def draw_chan_list(key, part):
    order_now = station_order(key)
    inverse = jnp.zeros((STATIONS,), jnp.int32).at[order_now].set(jnp.arange(STATIONS, dtype=jnp.int32))
    device_keys = jax.random.split(jax.random.fold_in(key, 23), N_TPL * N_STA)
    shuffles = jax.vmap(lambda one_key: jax.random.permutation(one_key, TPL_GRP * SL_DEV))(device_keys)
    owners = (shuffles // CAP).astype(jnp.int32).reshape(N_TPL, N_STA, TPL_GRP, SL_DEV)
    offset = jax.random.randint(jax.random.fold_in(key, 29), owners.shape, 0, STA_DEV).astype(jnp.int32)
    component = jax.random.randint(jax.random.fold_in(key, 31), owners.shape, 0, 3).astype(jnp.int32)
    station = inverse[owners * STA_DEV + offset]
    channel = 3 * station + component
    return jnp.transpose(channel, (0, 2, 1, 3)).reshape(TEMPLATES, SLOTS).astype(jnp.int32)


def draw_chan_count(key, part):
    lowest = SLOTS // 6
    highest = SLOTS * 15 // 16
    counts = jax.random.randint(jax.random.fold_in(key, 41), (TEMPLATES,), lowest, highest + 1).astype(jnp.int32)
    where_max = jax.random.randint(jax.random.fold_in(key, 43), (), 0, TEMPLATES)
    where_min = (where_max + 1 + jax.random.randint(jax.random.fold_in(key, 47), (), 0, TEMPLATES - 1)) % TEMPLATES
    counts = counts.at[where_max].set(highest)
    counts = counts.at[where_min].set(lowest)
    return counts.astype(jnp.int32)


def block_scale(own_key, extent, pieces, smallest, high):
    factor_of = 1.0
    for dim, blocks in pieces:
        draws = jax.random.uniform(jax.random.fold_in(jax.random.fold_in(own_key, 6), dim), (blocks,), jnp.float32, smallest / len(pieces), high / len(pieces))
        factor_of = factor_of * jnp.repeat(jnp.exp(draws), extent[dim] // blocks).reshape((-1,) + (1,) * (len(extent) - 1 - dim))
    return factor_of


def gaussian(stream_key, extent, scale, limit, cuts=(), held_as=jnp.bfloat16):
    entries = jax.random.normal(stream_key, extent, jnp.float32) * scale
    if len(cuts) > 0:
        entries = block_scale(stream_key, extent, cuts, -0.22, 0.18) * entries
    return jnp.clip(entries, min=-limit, max=limit).astype(held_as)


def setup_inputs(seed: int = 0) -> dict:
    splits = jax.random.split(jax.random.key(seed), 7)
    return {
        "window": gaussian(splits[0], (CHANNELS, LAGS), 1.0, 6.0, ((0, 8), (1, 4))),
        "prior": gaussian(splits[1], (CHANNELS, TLEN - 1), 1.0, 6.0, ((0, 8),)),
        "waves": gaussian(splits[2], (TEMPLATES, SLOTS, TLEN), 1.0, 6.0, ((0, 4), (1, 8))),
        "chan_list": draw_chan_list(jax.random.fold_in(splits[6], 71), 0),
        "chan_count": draw_chan_count(jax.random.fold_in(splits[6], 71), 0),
        "station_row": draw_station_row(jax.random.fold_in(splits[6], 71), 0),
    }


epsilon = 1e-06

def correlate(data_rows, wave_rows):
    result = lax.conv_general_dilated(data_rows[None], wave_rows[:, None, :], (1,), 'VALID', dimension_numbers=('NCH', 'OIH', 'NCH'), feature_group_count=data_rows.shape[0], preferred_element_type=jnp.float32)
    return result[0]

def inverse_energy(rows, lag_count, length):
    squares = rows.astype(jnp.float32) ** 2
    prefix = jnp.concatenate([jnp.zeros((rows.shape[0], 1), jnp.float32), jnp.cumsum(squares, axis=1)], axis=1)
    energy = prefix[:, length:length + lag_count] - prefix[:, :lag_count]
    return 1.0 / jnp.sqrt(energy + epsilon)

def unit_waves(waves, listed):
    raw_wave = waves.astype(jnp.float32)
    wave_norms = jnp.sqrt(lax.optimization_barrier(jnp.sum(raw_wave * raw_wave, axis=-1, keepdims=True)) + epsilon)
    return (raw_wave / wave_norms * listed[..., None]).astype(jnp.bfloat16)

def reference(window, prior, waves, chan_list, chan_count, station_row):
    extended = jnp.concatenate([prior, window], axis=1)
    scales = inverse_energy(extended, LAGS, TLEN)
    listed = (jnp.arange(SLOTS, dtype=jnp.int32)[None, :] < chan_count[:, None]).astype(jnp.float32)
    normed = unit_waves(waves, listed)
    rows_of = (3 * station_row[chan_list // 3] + chan_list % 3).astype(jnp.int32)

    def one_template(inputs):
        rows_here, waves_here = inputs
        traces = correlate(extended[rows_here], waves_here) * scales[rows_here]
        return lax.optimization_barrier(jnp.sum(traces, axis=0))
    return lax.map(one_template, (rows_of, normed))
```

```python
import functools

import jax
import jax.numpy as jnp
from jax import lax
from jax.experimental import pallas as pl
from jax.experimental.pallas import tpu as pltpu
from jax.sharding import PartitionSpec as P

epsilon = 1e-06
LANE = 128
STEP = 32
GROUP = 8
TURNS = LANE // STEP
F32, BF16, I32 = jnp.float32, jnp.bfloat16, jnp.int32


def up(value, unit):
    return -(-value // unit) * unit


def column_sum(values):
    return jnp.sum(values, axis=1, keepdims=True)


def route_kernel(
    sta_size, block_rows, sta_pos, waves, chan_list, chan_count, station_row, sent, padded
):
    positions, length = waves.shape
    group_size, slot_count = chan_list.shape
    width = sent.shape[1]
    capacity = positions // sta_size
    spot = lax.broadcasted_iota(I32, (positions, 1), 0)
    template = spot // slot_count
    slot = spot % slot_count
    slot_lane = lax.broadcasted_iota(I32, (positions, slot_count), 1)
    named = jnp.zeros((positions, slot_count), I32)
    count = jnp.zeros((positions, 1), I32)
    for t in range(group_size):
        here = template == t
        named = jnp.where(here, chan_list[t : t + 1, :], named)
        count = jnp.where(here, chan_count[t], count)
    channel = column_sum(jnp.where(slot_lane == slot, named.astype(F32), 0.0)).astype(I32)
    station = (channel * 21846) >> 16
    part = channel - 3 * station
    station_lane = lax.broadcasted_iota(I32, (positions, station_row.shape[1]), 1)
    found = column_sum(jnp.where(station_lane == station, station_row[...].astype(F32), 0.0))
    data_row = 3 * found.astype(I32) + part
    owner = jnp.zeros((positions, 1), I32)
    for o in range(1, sta_size):
        owner = owner + (data_row >= o * block_rows).astype(I32)
    local_row = data_row - owner * block_rows
    lane = lax.broadcasted_iota(I32, (positions, LANE), 1)
    row = lax.broadcasted_iota(I32, (positions, LANE), 0)
    hits = (lane == owner).astype(F32)
    before = (lane < row).astype(BF16)
    ahead = jnp.dot(before, hits.astype(BF16), preferred_element_type=F32)
    place = owner * capacity + column_sum(ahead * hits).astype(I32)
    goes = (lane == place).astype(F32).astype(BF16)

    padded[:, width - LANE :] = jnp.zeros((positions, LANE), F32)
    padded[:, :length] = waves[...].astype(F32)
    raw = padded[...]
    listed = (sta_pos[0] * slot_count + slot < count).astype(F32)
    gain = listed / jnp.sqrt(column_sum(raw * raw) + epsilon)
    wide = lax.broadcasted_iota(I32, (positions, width), 1)
    tagged = jnp.where(
        wide == length,
        local_row.astype(F32),
        jnp.where(wide == length + 1, (template ^ owner).astype(F32), raw * gain),
    ).astype(BF16)
    sent[...] = lax.dot_general(
        goes, tagged, (((0,), (0,)), ((), ())), preferred_element_type=F32
    ).astype(BF16)


def prepare_kernel(length, prior, window, shifted, scales, extended):
    rows, before = prior.shape
    lags = window.shape[1]
    total = extended.shape[1]
    start = before // LANE * LANE
    extended[:, :start] = jnp.zeros((rows, start), F32)
    extended[:, start:] = jnp.zeros((rows, total - start), F32)
    extended[:, start : start + lags] = window[...].astype(F32)
    moved = pltpu.roll(extended[:, start:], before - start, axis=1)
    extended[:, start:] = jnp.zeros((rows, total - start), F32)
    extended[:, :before] = prior[...].astype(F32)
    extended[:, start:] = extended[:, start:] + moved
    whole = extended[...]
    used = shifted.shape[2]
    for q in range(2):
        for h in range(2):
            shift = (2 * q + h) * STEP
            turned = whole if shift == 0 else pltpu.roll(whole, total - shift, axis=1)
            shifted[q, h * rows : (h + 1) * rows, :] = turned[:, :used].astype(BF16)
    square = whole * whole
    high = square.astype(BF16)
    low = (square - high.astype(F32)).astype(BF16)
    span = up(length + LANE - 1, LANE)
    sample = lax.broadcasted_iota(I32, (span, LANE), 0)
    lag = lax.broadcasted_iota(I32, (span, LANE), 1)
    band = ((sample >= lag) & (sample < lag + length)).astype(F32).astype(BF16)
    for a in range(lags // LANE):
        at = slice(a * LANE, a * LANE + span)
        energy = jnp.dot(high[:, at], band, preferred_element_type=F32) + jnp.dot(
            low[:, at], band, preferred_element_type=F32
        )
        scale = 1.0 / jnp.sqrt(energy + epsilon)
        for c in range(TURNS):
            turned = scale if c == 0 else pltpu.roll(scale, c * STEP, axis=1)
            turned_high = turned.astype(BF16)
            at = slice(c * rows, (c + 1) * rows)
            scales[at, a * LANE : (a + 1) * LANE] = turned_high
            scales[at, lags + a * LANE : lags + (a + 1) * LANE] = (
                turned - turned_high.astype(F32)
            ).astype(BF16)


def correlate_kernel(length, arrived, shifted, scales, kept, given, frames, waves, traces, toeplitz):
    positions, width = arrived.shape
    rows = scales.shape[0] // TURNS
    lags = scales.shape[1] // 2
    used = shifted.shape[2]
    blocks = lags // LANE
    waves[...] = arrived[...].astype(F32)
    wanted = waves[:, length : length + 1].astype(I32)
    template = waves[:, length + 1 : length + 2].astype(I32)
    turn = lax.broadcasted_iota(I32, (positions, 1), 0) % TURNS
    scale_lane = lax.broadcasted_iota(I32, (positions, TURNS * rows), 1)
    picks = (scale_lane == turn * rows + wanted).astype(F32).astype(BF16)
    group_size = 2 * kept.shape[0]
    lane = lax.broadcasted_iota(I32, (positions, TURNS * group_size), 1)
    chosen = (lane == turn * group_size + template).astype(F32).astype(BF16)

    pairs = wanted.reshape(positions // GROUP, GROUP, 1)
    twice = jnp.concatenate([pairs, pairs + rows], axis=1).reshape(2 * positions, 1)
    picks_twice = (
        (lax.broadcasted_iota(I32, (2 * positions, 2 * rows), 1) == twice).astype(F32).astype(BF16)
    )
    for q in range(2):
        frames[q] = jnp.dot(picks_twice, shifted[q], preferred_element_type=F32).astype(BF16)
    traces[...] = jnp.dot(picks, scales[:, :lags], preferred_element_type=F32) + jnp.dot(
        picks, scales[:, lags:], preferred_element_type=F32
    )
    waves[:, width - LANE :] = jnp.where(
        lax.broadcasted_iota(I32, (positions, LANE), 1) < length - (width - LANE),
        waves[:, width - LANE :],
        0.0,
    )
    low_half = lax.broadcasted_iota(I32, (blocks * GROUP, LANE), 0) % GROUP < GROUP // 2
    lane_block = lax.broadcasted_iota(I32, (blocks * GROUP, LANE), 1) // STEP
    lane_block = (
        lane_block + TURNS - lax.broadcasted_iota(I32, (blocks * GROUP, LANE), 0) % TURNS
    ) % TURNS

    def one_group(g, _):
        first = pl.multiple_of(g * GROUP, GROUP)
        for j in range(GROUP):
            wave = jnp.broadcast_to(waves[pl.ds(first + j, 1), :], (STEP, width))
            toeplitz[j * STEP : (j + 1) * STEP, :] = pltpu.roll(
                wave, 0, axis=1, stride=1, stride_axis=0
            ).astype(BF16)
        at = pl.ds(pl.multiple_of(g * 2 * GROUP, 2 * GROUP), 2 * GROUP)
        data = [
            frames[q, at, a * LANE : a * LANE + width] for q in range(2) for a in range(blocks)
        ]
        product = lax.dot_general(
            jnp.concatenate(data, axis=0),
            toeplitz[...],
            (((1,), (1,)), ((), ())),
            preferred_element_type=F32,
        )
        product = product.reshape(2, blocks, 2, GROUP, 2 * LANE)
        own = jnp.zeros((blocks * GROUP, LANE), F32)
        for q in range(2):
            for h in range(2):
                part = product[q, :, h].reshape(blocks * GROUP, 2 * LANE)
                part = jnp.where(low_half, part[:, :LANE], part[:, LANE:])
                step = 2 * q + h
                if step > 0:
                    part = pltpu.roll(part, step * STEP, axis=1)
                own = jnp.where(lane_block == step, part, own)
        own = own.reshape(blocks, GROUP, LANE)
        for a in range(blocks):
            at_lag = slice(a * LANE, (a + 1) * LANE)
            traces[pl.ds(first, GROUP), at_lag] = traces[pl.ds(first, GROUP), at_lag] * own[a]
        return 0

    lax.fori_loop(0, positions // GROUP, one_group, 0)
    scaled = traces[...]
    high = scaled.astype(BF16)
    low = (scaled - high.astype(F32)).astype(BF16)
    by_template = (((0,), (0,)), ((), ()))
    stacked = lax.dot_general(
        chosen, high, by_template, preferred_element_type=F32
    ) + lax.dot_general(chosen, low, by_template, preferred_element_type=F32)
    for a in range(blocks):
        at_lag = slice(a * LANE, (a + 1) * LANE)
        total = stacked[:group_size, at_lag]
        for c in range(1, TURNS):
            part = stacked[c * group_size : (c + 1) * group_size, at_lag]
            total = total + pltpu.roll(part, LANE - c * STEP, axis=1)
        kept[:, at_lag] = total[: group_size // 2]
        given[:, at_lag] = total[group_size // 2 :]


def per_device(window, prior, waves, chan_list, chan_count, station_row):
    sta_size = lax.axis_size("sta")
    sta_pos = lax.axis_index("sta").astype(I32).reshape(1)
    group_size, slot_count, length = waves.shape
    positions = group_size * slot_count
    block_rows = prior.shape[0]
    width = up(length + STEP, LANE)
    lags = window.shape[1] * lax.axis_size("tpl")
    vmem = pl.BlockSpec(memory_space=pltpu.VMEM)
    smem = pl.BlockSpec(memory_space=pltpu.SMEM)

    sent = pl.pallas_call(
        functools.partial(route_kernel, sta_size, block_rows),
        out_shape=jax.ShapeDtypeStruct((positions, width), BF16),
        in_specs=[smem, vmem, vmem, smem, vmem],
        out_specs=vmem,
        scratch_shapes=[pltpu.VMEM((positions, width), F32)],
        name="route",
    )(
        sta_pos,
        waves.reshape(positions, length),
        chan_list,
        chan_count,
        station_row.reshape(1, station_row.shape[0]),
    )
    arrived = lax.all_to_all(
        sent.reshape(sta_size, positions // sta_size, width),
        "sta",
        split_axis=0,
        concat_axis=0,
        tiled=True,
    ).reshape(positions, width)

    whole_time = lax.all_gather(window, "tpl", axis=1, tiled=True)
    total = up(prior.shape[1] + lags, LANE)
    used = lags - LANE + width
    shifted, scales = pl.pallas_call(
        functools.partial(prepare_kernel, length),
        out_shape=[
            jax.ShapeDtypeStruct((2, 2 * block_rows, used), BF16),
            jax.ShapeDtypeStruct((TURNS * block_rows, 2 * lags), BF16),
        ],
        in_specs=[vmem, vmem],
        out_specs=[vmem, vmem],
        scratch_shapes=[pltpu.VMEM((block_rows, total), F32)],
        name="prepare",
    )(prior, whole_time)

    half = group_size // 2
    kept, given = pl.pallas_call(
        functools.partial(correlate_kernel, length),
        out_shape=[jax.ShapeDtypeStruct((half, lags), F32)] * 2,
        in_specs=[vmem] * 3,
        out_specs=[vmem] * 2,
        scratch_shapes=[
            pltpu.VMEM((2, 2 * positions, used), BF16),
            pltpu.VMEM((positions, width), F32),
            pltpu.VMEM((positions, lags), F32),
            pltpu.VMEM((GROUP * STEP, width), BF16),
        ],
        compiler_params=pltpu.CompilerParams(vmem_limit_bytes=32 * 1024 * 1024),
        name="correlate",
    )(arrived, shifted, scales)

    distance = sta_size // 2
    while True:
        pairs = [(i, i ^ distance) for i in range(sta_size)]
        kept = kept + lax.ppermute(given, "sta", pairs)
        if distance == 1:
            return kept
        distance //= 2
        kept, given = kept[:distance], kept[distance:]


def solution(mesh):
    in_specs = (
        P("sta", "tpl"),
        P("sta", None),
        P("tpl", "sta", None),
        P("tpl", "sta"),
        P("tpl"),
        P(),
    )
    out_specs = P(("tpl", "sta"), None)
    return jax.shard_map(
        per_device, mesh=mesh, in_specs=in_specs, out_specs=out_specs, check_vma=False
    )
```

```python
import functools

import jax
import jax.numpy as jnp
from jax import lax
from jax.experimental import pallas as pl
from jax.experimental.pallas import tpu as pltpu
from jax.sharding import PartitionSpec as P

epsilon = 1e-06
LANE = 128
STEP = 32
GROUP = 8
TURNS = LANE // STEP
MIB = 1 << 20
F32, BF16, I32 = jnp.float32, jnp.bfloat16, jnp.int32


def up(value, unit):
    return -(-value // unit) * unit


def column_sum(values):
    return jnp.sum(values, axis=1, keepdims=True)


def route_kernel(
    sta_size, block_rows, sta_pos, waves, chan_list, chan_count, station_row, sent, padded
):
    positions, length = waves.shape
    group_size, slot_count = chan_list.shape
    width = sent.shape[1]
    capacity = positions // sta_size
    spot = lax.broadcasted_iota(I32, (positions, 1), 0)
    template = spot // slot_count
    slot = spot % slot_count
    slot_lane = lax.broadcasted_iota(I32, (positions, slot_count), 1)
    named = jnp.zeros((positions, slot_count), I32)
    count = jnp.zeros((positions, 1), I32)
    for t in range(group_size):
        here = template == t
        named = jnp.where(here, chan_list[t : t + 1, :], named)
        count = jnp.where(here, chan_count[t], count)
    channel = column_sum(jnp.where(slot_lane == slot, named.astype(F32), 0.0)).astype(I32)
    station = (channel * 21846) >> 16
    part = channel - 3 * station
    station_lane = lax.broadcasted_iota(I32, (positions, station_row.shape[1]), 1)
    found = column_sum(jnp.where(station_lane == station, station_row[...].astype(F32), 0.0))
    data_row = 3 * found.astype(I32) + part
    owner = jnp.zeros((positions, 1), I32)
    for o in range(1, sta_size):
        owner = owner + (data_row >= o * block_rows).astype(I32)
    local_row = data_row - owner * block_rows
    lane = lax.broadcasted_iota(I32, (positions, LANE), 1)
    row = lax.broadcasted_iota(I32, (positions, LANE), 0)
    hits = (lane == owner).astype(F32)
    before = (lane < row).astype(BF16)
    ahead = jnp.dot(before, hits.astype(BF16), preferred_element_type=F32)
    place = owner * capacity + column_sum(ahead * hits).astype(I32)
    goes = (lane == place).astype(F32).astype(BF16)

    padded[:, width - LANE :] = jnp.zeros((positions, LANE), F32)
    padded[:, :length] = waves[...].astype(F32)
    raw = padded[...]
    listed = (sta_pos[0] * slot_count + slot < count).astype(F32)
    gain = listed / jnp.sqrt(column_sum(raw * raw) + epsilon)
    wide = lax.broadcasted_iota(I32, (positions, width), 1)
    tagged = jnp.where(
        wide == length,
        local_row.astype(F32),
        jnp.where(wide == length + 1, (template ^ owner).astype(F32), raw * gain),
    ).astype(BF16)
    sent[...] = lax.dot_general(
        goes, tagged, (((0,), (0,)), ((), ())), preferred_element_type=F32
    ).astype(BF16)


def prepare_kernel(length, prior, window, shifted, scales, extended):
    rows, before = prior.shape
    lags = window.shape[1]
    total = extended.shape[1]
    start = before // LANE * LANE
    extended[:, :start] = jnp.zeros((rows, start), F32)
    extended[:, start:] = jnp.zeros((rows, total - start), F32)
    extended[:, start : start + lags] = window[...].astype(F32)
    moved = pltpu.roll(extended[:, start:], before - start, axis=1)
    extended[:, start:] = jnp.zeros((rows, total - start), F32)
    extended[:, :before] = prior[...].astype(F32)
    extended[:, start:] = extended[:, start:] + moved
    whole = extended[...]
    used = shifted.shape[2]
    for q in range(2):
        for h in range(2):
            shift = (2 * q + h) * STEP
            turned = whole if shift == 0 else pltpu.roll(whole, total - shift, axis=1)
            shifted[q, h * rows : (h + 1) * rows, :] = turned[:, :used].astype(BF16)
    square = whole * whole
    high = square.astype(BF16)
    low = (square - high.astype(F32)).astype(BF16)
    span = up(length + LANE - 1, LANE)
    sample = lax.broadcasted_iota(I32, (span, LANE), 0)
    lag = lax.broadcasted_iota(I32, (span, LANE), 1)
    band = ((sample >= lag) & (sample < lag + length)).astype(F32).astype(BF16)
    for a in range(lags // LANE):
        at = slice(a * LANE, a * LANE + span)
        energy = jnp.dot(high[:, at], band, preferred_element_type=F32) + jnp.dot(
            low[:, at], band, preferred_element_type=F32
        )
        scale = 1.0 / jnp.sqrt(energy + epsilon)
        for c in range(TURNS):
            turned = scale if c == 0 else pltpu.roll(scale, c * STEP, axis=1)
            turned_high = turned.astype(BF16)
            at = slice(c * rows, (c + 1) * rows)
            scales[at, a * LANE : (a + 1) * LANE] = turned_high
            scales[at, lags + a * LANE : lags + (a + 1) * LANE] = (
                turned - turned_high.astype(F32)
            ).astype(BF16)


def correlate_kernel(length, arrived, shifted, scales, kept, given, frames, waves, traces, toeplitz):
    positions, width = arrived.shape
    rows = scales.shape[0] // TURNS
    lags = scales.shape[1] // 2
    used = shifted.shape[2]
    blocks = lags // LANE
    waves[...] = arrived[...].astype(F32)
    wanted = waves[:, length : length + 1].astype(I32)
    template = waves[:, length + 1 : length + 2].astype(I32)
    turn = lax.broadcasted_iota(I32, (positions, 1), 0) % TURNS
    scale_lane = lax.broadcasted_iota(I32, (positions, TURNS * rows), 1)
    picks = (scale_lane == turn * rows + wanted).astype(F32).astype(BF16)
    group_size = 2 * kept.shape[0]
    lane = lax.broadcasted_iota(I32, (positions, TURNS * group_size), 1)
    chosen = (lane == turn * group_size + template).astype(F32).astype(BF16)

    pairs = wanted.reshape(positions // GROUP, GROUP, 1)
    twice = jnp.concatenate([pairs, pairs + rows], axis=1).reshape(2 * positions, 1)
    picks_twice = (
        (lax.broadcasted_iota(I32, (2 * positions, 2 * rows), 1) == twice).astype(F32).astype(BF16)
    )
    for q in range(2):
        frames[q] = jnp.dot(picks_twice, shifted[q], preferred_element_type=F32).astype(BF16)
    traces[...] = jnp.dot(picks, scales[:, :lags], preferred_element_type=F32) + jnp.dot(
        picks, scales[:, lags:], preferred_element_type=F32
    )
    waves[:, width - LANE :] = jnp.where(
        lax.broadcasted_iota(I32, (positions, LANE), 1) < length - (width - LANE),
        waves[:, width - LANE :],
        0.0,
    )
    low_half = lax.broadcasted_iota(I32, (blocks * GROUP, LANE), 0) % GROUP < GROUP // 2
    lane_block = lax.broadcasted_iota(I32, (blocks * GROUP, LANE), 1) // STEP
    lane_block = (
        lane_block + TURNS - lax.broadcasted_iota(I32, (blocks * GROUP, LANE), 0) % TURNS
    ) % TURNS

    def one_group(g, _):
        first = pl.multiple_of(g * GROUP, GROUP)
        for j in range(GROUP):
            wave = jnp.broadcast_to(waves[pl.ds(first + j, 1), :], (STEP, width))
            toeplitz[j * STEP : (j + 1) * STEP, :] = pltpu.roll(
                wave, 0, axis=1, stride=1, stride_axis=0
            ).astype(BF16)
        at = pl.ds(pl.multiple_of(g * 2 * GROUP, 2 * GROUP), 2 * GROUP)
        data = [
            frames[q, at, a * LANE : a * LANE + width] for q in range(2) for a in range(blocks)
        ]
        product = lax.dot_general(
            jnp.concatenate(data, axis=0),
            toeplitz[...],
            (((1,), (1,)), ((), ())),
            preferred_element_type=F32,
        )
        product = product.reshape(2, blocks, 2, GROUP, 2 * LANE)
        own = jnp.zeros((blocks * GROUP, LANE), F32)
        for q in range(2):
            for h in range(2):
                part = product[q, :, h].reshape(blocks * GROUP, 2 * LANE)
                part = jnp.where(low_half, part[:, :LANE], part[:, LANE:])
                step = 2 * q + h
                if step > 0:
                    part = pltpu.roll(part, step * STEP, axis=1)
                own = jnp.where(lane_block == step, part, own)
        own = own.reshape(blocks, GROUP, LANE)
        for a in range(blocks):
            at_lag = slice(a * LANE, (a + 1) * LANE)
            traces[pl.ds(first, GROUP), at_lag] = traces[pl.ds(first, GROUP), at_lag] * own[a]
        return 0

    lax.fori_loop(0, positions // GROUP, one_group, 0, unroll=True)
    scaled = traces[...]
    high = scaled.astype(BF16)
    low = (scaled - high.astype(F32)).astype(BF16)
    by_template = (((0,), (0,)), ((), ()))
    stacked = lax.dot_general(
        chosen, high, by_template, preferred_element_type=F32
    ) + lax.dot_general(chosen, low, by_template, preferred_element_type=F32)
    for a in range(blocks):
        at_lag = slice(a * LANE, (a + 1) * LANE)
        total = stacked[:group_size, at_lag]
        for c in range(1, TURNS):
            part = stacked[c * group_size : (c + 1) * group_size, at_lag]
            total = total + pltpu.roll(part, LANE - c * STEP, axis=1)
        kept[:, at_lag] = total[: group_size // 2]
        given[:, at_lag] = total[group_size // 2 :]


def per_device(window, prior, waves, chan_list, chan_count, station_row):
    sta_size = lax.axis_size("sta")
    sta_pos = lax.axis_index("sta").astype(I32).reshape(1)
    group_size, slot_count, length = waves.shape
    positions = group_size * slot_count
    block_rows = prior.shape[0]
    width = up(length + STEP, LANE)
    lags = window.shape[1] * lax.axis_size("tpl")
    vmem = pl.BlockSpec(memory_space=pltpu.VMEM)
    smem = pl.BlockSpec(memory_space=pltpu.SMEM)

    sent = pl.pallas_call(
        functools.partial(route_kernel, sta_size, block_rows),
        out_shape=jax.ShapeDtypeStruct((positions, width), BF16),
        in_specs=[smem, vmem, vmem, smem, vmem],
        out_specs=vmem,
        scratch_shapes=[pltpu.VMEM((positions, width), F32)],
        compiler_params=pltpu.CompilerParams(vmem_limit_bytes=8 * MIB),
        name="route",
    )(
        sta_pos,
        waves.reshape(positions, length),
        chan_list,
        chan_count,
        station_row.reshape(1, station_row.shape[0]),
    )
    arrived = lax.all_to_all(
        sent.reshape(sta_size, positions // sta_size, width),
        "sta",
        split_axis=0,
        concat_axis=0,
        tiled=True,
    ).reshape(positions, width)

    whole_time = lax.all_gather(window, "tpl", axis=1, tiled=True)
    total = up(prior.shape[1] + lags, LANE)
    used = lags - LANE + width
    shifted, scales = pl.pallas_call(
        functools.partial(prepare_kernel, length),
        out_shape=[
            jax.ShapeDtypeStruct((2, 2 * block_rows, used), BF16),
            jax.ShapeDtypeStruct((TURNS * block_rows, 2 * lags), BF16),
        ],
        in_specs=[vmem, vmem],
        out_specs=[vmem, vmem],
        scratch_shapes=[pltpu.VMEM((block_rows, total), F32)],
        compiler_params=pltpu.CompilerParams(vmem_limit_bytes=16 * MIB),
        name="prepare",
    )(prior, whole_time)

    half = group_size // 2
    kept, given = pl.pallas_call(
        functools.partial(correlate_kernel, length),
        out_shape=[jax.ShapeDtypeStruct((half, lags), F32)] * 2,
        in_specs=[vmem] * 3,
        out_specs=[vmem] * 2,
        scratch_shapes=[
            pltpu.VMEM((2, 2 * positions, used), BF16),
            pltpu.VMEM((positions, width), F32),
            pltpu.VMEM((positions, lags), F32),
            pltpu.VMEM((GROUP * STEP, width), BF16),
        ],
        compiler_params=pltpu.CompilerParams(vmem_limit_bytes=16 * MIB),
        name="correlate",
    )(arrived, shifted, scales)

    distance = sta_size // 2
    while True:
        pairs = [(i, i ^ distance) for i in range(sta_size)]
        kept = kept + lax.ppermute(given, "sta", pairs)
        if distance == 1:
            return kept
        distance //= 2
        kept, given = kept[:distance], kept[distance:]


def solution(mesh):
    in_specs = (
        P("sta", "tpl"),
        P("sta", None),
        P("tpl", "sta", None),
        P("tpl", "sta"),
        P("tpl"),
        P(),
    )
    out_specs = P(("tpl", "sta"), None)
    return jax.shard_map(
        per_device, mesh=mesh, in_specs=in_specs, out_specs=out_specs, check_vma=False
    )
```

```python
import functools

import jax
import jax.numpy as jnp
from jax import lax
from jax.experimental import pallas as pl
from jax.experimental.pallas import tpu as pltpu
from jax.sharding import PartitionSpec as P

epsilon = 1e-06
LANE = 128
STEP = 32
GROUP = 8
CHUNK = 1
TURNS = LANE // STEP
MIB = 1 << 20
F32, BF16, I32 = jnp.float32, jnp.bfloat16, jnp.int32


def up(value, unit):
    return -(-value // unit) * unit


def column_sum(values):
    return jnp.sum(values, axis=1, keepdims=True)


def route_kernel(
    sta_size,
    block_rows,
    sta_pos,
    waves_in,
    chan_list_in,
    chan_count_in,
    station_row_in,
    sent,
    waves,
    chan_list,
    chan_count,
    station_row,
    channels,
    padded,
    arrivals,
):
    copies = [
        pltpu.make_async_copy(source, target, arrivals.at[i])
        for i, (source, target) in enumerate(
            (
                (chan_list_in, chan_list),
                (station_row_in, station_row),
                (chan_count_in, chan_count),
                (waves_in, waves),
            )
        )
    ]
    for copy in copies:
        copy.start()
    positions, length = waves.shape
    group_size, slot_count = chan_list.shape
    width = sent.shape[1]
    capacity = positions // sta_size
    padded[:, width - LANE :] = jnp.zeros((positions, LANE), F32)
    channels[...] = jnp.zeros(channels.shape, I32)
    row = lax.broadcasted_iota(I32, (positions, positions), 0)
    lane = lax.broadcasted_iota(I32, (positions, positions), 1)
    before = (row < lane).astype(F32).astype(BF16)
    spot = lax.broadcasted_iota(I32, (positions, 1), 0)
    slot = sta_pos[0] * slot_count + spot % slot_count
    along = lax.broadcasted_iota(I32, (1, positions), 1)
    for copy in copies[:3]:
        copy.wait()

    channels[:, :slot_count] = chan_list[...]
    channel = channels[...]
    station = (channel * 21846) >> 16
    found = jnp.zeros(channel.shape, I32)
    for first in range(0, station_row.shape[1], LANE):
        some = jnp.broadcast_to(station_row[:, first : first + LANE], channel.shape)
        place = jnp.clip(station - first, 0, LANE - 1)
        here = (station >= first) & (station < first + LANE)
        found = jnp.where(here, jnp.take_along_axis(some, place, axis=1), found)
    data_row = 3 * found + channel - 3 * station
    spread = jnp.where(lax.broadcasted_iota(I32, channel.shape, 1) < slot_count, data_row, 0)
    spread = pltpu.roll(spread.astype(F32), 0, axis=1, stride=slot_count, stride_axis=0)
    data_row = jnp.sum(spread, axis=0, keepdims=True).astype(I32)
    owner = jnp.zeros((1, positions), I32)
    for o in range(1, sta_size):
        owner = owner + (data_row >= o * block_rows).astype(I32)
    local_row = data_row - owner * block_rows
    relative = along // slot_count ^ owner
    hits = (lax.broadcasted_iota(I32, (sta_size, positions), 0) == owner).astype(F32)
    ahead = jnp.dot(hits.astype(BF16), before, preferred_element_type=F32)
    rank = jnp.sum(ahead * hits, axis=0, keepdims=True).astype(I32)
    goes = row == owner * capacity + rank
    row_tag = column_sum(jnp.where(goes, local_row, 0).astype(F32))
    template_tag = column_sum(jnp.where(goes, relative, 0).astype(F32))

    count = jnp.zeros((positions, 1), I32)
    for t in range(group_size):
        count = jnp.where(spot // slot_count == t, chan_count[t], count)
    copies[3].wait()
    padded[:, :length] = waves[...].astype(F32)
    raw = padded[...]
    listed = (slot < count).astype(F32)
    gain = listed / jnp.sqrt(column_sum(raw * raw) + epsilon)
    ordered = jnp.dot(
        goes.astype(F32).astype(BF16), (raw * gain).astype(BF16), preferred_element_type=F32
    )
    wide = lax.broadcasted_iota(I32, (positions, width), 1)
    sent[...] = jnp.where(
        wide == length, row_tag, jnp.where(wide == length + 1, template_tag, ordered)
    ).astype(BF16)


def prepare_kernel(length, prior, window, shifted, scales, extended):
    rows, before = prior.shape
    lags = window.shape[1]
    total = extended.shape[1]
    start = before // LANE * LANE
    extended[:, :start] = jnp.zeros((rows, start), F32)
    extended[:, start:] = jnp.zeros((rows, total - start), F32)
    extended[:, start : start + lags] = window[...].astype(F32)
    moved = pltpu.roll(extended[:, start:], before - start, axis=1)
    extended[:, start:] = jnp.zeros((rows, total - start), F32)
    extended[:, :before] = prior[...].astype(F32)
    extended[:, start:] = extended[:, start:] + moved
    whole = extended[...]
    used = shifted.shape[1]
    for turn in range(TURNS):
        moved = whole if turn == 0 else pltpu.roll(whole, total - turn * STEP, axis=1)
        shifted[turn * rows : (turn + 1) * rows, :] = moved[:, :used].astype(BF16)
    square = whole * whole
    high = square.astype(BF16)
    low = (square - high.astype(F32)).astype(BF16)
    span = up(length + LANE - 1, LANE)
    sample = lax.broadcasted_iota(I32, (span, LANE), 0)
    lag = lax.broadcasted_iota(I32, (span, LANE), 1)
    band = ((sample >= lag) & (sample < lag + length)).astype(F32).astype(BF16)
    for a in range(lags // LANE):
        at = slice(a * LANE, a * LANE + span)
        energy = jnp.dot(high[:, at], band, preferred_element_type=F32) + jnp.dot(
            low[:, at], band, preferred_element_type=F32
        )
        scale = 1.0 / jnp.sqrt(energy + epsilon)
        scale_high = scale.astype(BF16)
        scales[:rows, a * LANE : (a + 1) * LANE] = scale_high
        scales[rows:, a * LANE : (a + 1) * LANE] = (scale - scale_high.astype(F32)).astype(BF16)


def correlate_kernel(
    length, arrived, shifted, scales, kept, given, frames, waves, traces, toeplitz, sums
):
    positions, width = arrived.shape
    rows = scales.shape[0] // 2
    lags = scales.shape[1]
    half = kept.shape[0]
    blocks = lags // LANE
    waves[...] = arrived[...].astype(F32)
    wanted = waves[:, length : length + 1].astype(I32)
    template = jnp.broadcast_to(waves[:, length + 1 : length + 2].astype(I32), (positions, LANE))

    pairs = wanted.reshape(positions // GROUP, 1, GROUP, 1)
    twice = jnp.concatenate([pairs, pairs], axis=1).reshape(2 * positions, 1)
    place = lax.broadcasted_iota(I32, (2 * positions, 1), 0)
    moved = place // GROUP % 2 + place % GROUP
    every = lax.broadcasted_iota(I32, (2 * positions, TURNS * rows), 1)
    for q in range(2):
        picks = every == (2 * q + moved) % TURNS * rows + twice
        frames[q] = jnp.dot(
            picks.astype(F32).astype(BF16), shifted[...], preferred_element_type=F32
        ).astype(BF16)
    either = lax.broadcasted_iota(I32, (positions, 2 * rows), 1)
    picks = (either == wanted) | (either == wanted + rows)
    picks = picks.astype(F32).astype(BF16)
    waves[:, width - LANE :] = jnp.where(
        lax.broadcasted_iota(I32, (positions, LANE), 1) < length - (width - LANE),
        waves[:, width - LANE :],
        0.0,
    )
    shape = (blocks * GROUP, LANE)
    member = lax.broadcasted_iota(I32, shape, 0) % GROUP
    low_half = member < TURNS
    turn = (lax.broadcasted_iota(I32, shape, 1) // STEP + 2 * TURNS - member) % TURNS

    for g in range(positions // GROUP):
        first = g * GROUP
        copies = toeplitz.at[g % toeplitz.shape[0]]
        for j in range(GROUP):
            wave = jnp.broadcast_to(waves[first + j : first + j + 1, :], (STEP, width))
            copies[j * STEP : (j + 1) * STEP, :] = pltpu.roll(
                wave, 0, axis=1, stride=1, stride_axis=0
            ).astype(BF16)
        at = slice(g * 2 * GROUP, (g + 1) * 2 * GROUP)
        data = [
            frames[q, at, a * LANE : a * LANE + width] for q in range(2) for a in range(blocks)
        ]
        product = lax.dot_general(
            jnp.concatenate(data, axis=0),
            copies[...],
            (((1,), (1,)), ((), ())),
            preferred_element_type=F32,
        )
        if g == 0:
            traces[...] = jnp.dot(picks, scales[...], preferred_element_type=F32)
        product = product.reshape(2, blocks, 2, GROUP, 2 * LANE)
        own = jnp.zeros(shape, F32)
        for step in range(TURNS):
            part = product[step // 2, :, step % 2].reshape(blocks * GROUP, 2 * LANE)
            part = jnp.where(low_half, part[:, :LANE], part[:, LANE:])
            if step > 0:
                part = pltpu.roll(part, step * STEP, axis=1)
            own = jnp.where(turn == step, part, own)
        own = own.reshape(blocks, GROUP, LANE)
        for a in range(blocks):
            at_lag = slice(a * LANE, (a + 1) * LANE)
            traces[first : first + GROUP, at_lag] = traces[first : first + GROUP, at_lag] * own[a]
        if (g + 1) % CHUNK == 0:
            for t in range(2 * half):
                total = jnp.zeros((GROUP, lags), F32) if g + 1 == CHUNK else sums[t]
                for done in range(g + 1 - CHUNK, g + 1):
                    ready = slice(done * GROUP, (done + 1) * GROUP)
                    mine = (template[ready] == t).astype(F32)
                    total = total + traces[ready, :] * jnp.concatenate([mine] * blocks, axis=1)
                sums[t] = total
    stacked = jnp.sum(sums[...], axis=1)
    kept[...] = stacked[:half]
    given[...] = stacked[half:]


def per_device(window, prior, waves, chan_list, chan_count, station_row):
    sta_size = lax.axis_size("sta")
    sta_pos = lax.axis_index("sta").astype(I32).reshape(1)
    group_size, slot_count, length = waves.shape
    positions = group_size * slot_count
    block_rows = prior.shape[0]
    width = up(length + STEP, LANE)
    lags = window.shape[1] * lax.axis_size("tpl")
    vmem = pl.BlockSpec(memory_space=pltpu.VMEM)
    smem = pl.BlockSpec(memory_space=pltpu.SMEM)

    anywhere = pl.BlockSpec(memory_space=pl.ANY)
    sent = pl.pallas_call(
        functools.partial(route_kernel, sta_size, block_rows),
        out_shape=jax.ShapeDtypeStruct((positions, width), BF16),
        in_specs=[smem] + [anywhere] * 4,
        out_specs=vmem,
        scratch_shapes=[
            pltpu.VMEM((positions, length), BF16),
            pltpu.VMEM((group_size, slot_count), I32),
            pltpu.SMEM((group_size,), I32),
            pltpu.VMEM((1, station_row.shape[0]), I32),
            pltpu.VMEM((group_size, LANE), I32),
            pltpu.VMEM((positions, width), F32),
            pltpu.SemaphoreType.DMA((4,)),
        ],
        name="route",
    )(
        sta_pos,
        waves.reshape(positions, length),
        chan_list,
        chan_count,
        station_row.reshape(1, station_row.shape[0]),
    )
    arrived = lax.all_to_all(
        sent.reshape(sta_size, positions // sta_size, width),
        "sta",
        split_axis=0,
        concat_axis=0,
        tiled=True,
    ).reshape(positions, width)

    whole_time = lax.all_gather(window, "tpl", axis=1, tiled=True)
    total = up(prior.shape[1] + lags, LANE)
    used = lags - LANE + width
    shifted, scales = pl.pallas_call(
        functools.partial(prepare_kernel, length),
        out_shape=[
            jax.ShapeDtypeStruct((TURNS * block_rows, used), BF16),
            jax.ShapeDtypeStruct((2 * block_rows, lags), BF16),
        ],
        in_specs=[vmem, vmem],
        out_specs=[vmem, vmem],
        scratch_shapes=[pltpu.VMEM((block_rows, total), F32)],
        compiler_params=pltpu.CompilerParams(vmem_limit_bytes=16 * MIB),
        name="prepare",
    )(prior, whole_time)

    half = group_size // 2
    kept, given = pl.pallas_call(
        functools.partial(correlate_kernel, length),
        out_shape=[jax.ShapeDtypeStruct((half, lags), F32)] * 2,
        in_specs=[vmem] * 3,
        out_specs=[vmem] * 2,
        scratch_shapes=[
            pltpu.VMEM((2, 2 * positions, used), BF16),
            pltpu.VMEM((positions, width), F32),
            pltpu.VMEM((positions, lags), F32),
            pltpu.VMEM((positions // GROUP, GROUP * STEP, width), BF16),
            pltpu.VMEM((group_size, GROUP, lags), F32),
        ],
        compiler_params=pltpu.CompilerParams(vmem_limit_bytes=16 * MIB),
        name="correlate",
    )(arrived, shifted, scales)

    distance = sta_size // 2
    while True:
        pairs = [(i, i ^ distance) for i in range(sta_size)]
        kept = kept + lax.ppermute(given, "sta", pairs)
        if distance == 1:
            return kept
        distance //= 2
        kept, given = kept[:distance], kept[distance:]


def solution(mesh):
    in_specs = (
        P("sta", "tpl"),
        P("sta", None),
        P("tpl", "sta", None),
        P("tpl", "sta"),
        P("tpl"),
        P(),
    )
    out_specs = P(("tpl", "sta"), None)
    return jax.shard_map(
        per_device, mesh=mesh, in_specs=in_specs, out_specs=out_specs, check_vma=False
    )
```

```python
import functools

import jax
import jax.numpy as jnp
from jax import lax
from jax.experimental import pallas as pl
from jax.experimental.pallas import tpu as pltpu
from jax.sharding import PartitionSpec as P

epsilon = 1e-06
LANE = 128
STEP = 32
GROUP = 8
CHUNK = 1
TURNS = LANE // STEP
MIB = 1 << 20
F32, BF16, I32 = jnp.float32, jnp.bfloat16, jnp.int32


def up(value, unit):
    return -(-value // unit) * unit


def column_sum(values):
    return jnp.sum(values, axis=1, keepdims=True)


def half_way(place, size):
    return (place + size // 2) % size


def route_kernel(
    sta_size,
    block_rows,
    sta_pos,
    waves_in,
    chan_list_in,
    chan_count_in,
    station_row_in,
    sent,
    waves,
    chan_list,
    chan_count,
    station_row,
    channels,
    padded,
    arrivals,
):
    copies = [
        pltpu.make_async_copy(source, target, arrivals.at[i])
        for i, (source, target) in enumerate(
            (
                (chan_list_in, chan_list),
                (station_row_in, station_row),
                (chan_count_in, chan_count),
                (waves_in, waves),
            )
        )
    ]
    for copy in copies:
        copy.start()
    positions, length = waves.shape
    group_size, slot_count = chan_list.shape
    width = sent.shape[1]
    capacity = positions // sta_size
    padded[:, width - LANE :] = jnp.zeros((positions, LANE), F32)
    channels[...] = jnp.zeros(channels.shape, I32)
    row = lax.broadcasted_iota(I32, (positions, positions), 0)
    lane = lax.broadcasted_iota(I32, (positions, positions), 1)
    before = (row < lane).astype(F32).astype(BF16)
    spot = lax.broadcasted_iota(I32, (positions, 1), 0)
    slot = sta_pos[0] * slot_count + spot % slot_count
    along = lax.broadcasted_iota(I32, (1, positions), 1)
    for copy in copies[:3]:
        copy.wait()

    channels[:, :slot_count] = chan_list[...]
    channel = channels[...]
    station = (channel * 21846) >> 16
    found = jnp.zeros(channel.shape, I32)
    for first in range(0, station_row.shape[1], LANE):
        some = jnp.broadcast_to(station_row[:, first : first + LANE], channel.shape)
        place = jnp.clip(station - first, 0, LANE - 1)
        here = (station >= first) & (station < first + LANE)
        found = jnp.where(here, jnp.take_along_axis(some, place, axis=1), found)
    data_row = 3 * found + channel - 3 * station
    spread = jnp.where(lax.broadcasted_iota(I32, channel.shape, 1) < slot_count, data_row, 0)
    spread = pltpu.roll(spread.astype(F32), 0, axis=1, stride=slot_count, stride_axis=0)
    data_row = jnp.sum(spread, axis=0, keepdims=True).astype(I32)
    owner = jnp.zeros((1, positions), I32)
    for o in range(1, sta_size):
        owner = owner + (data_row >= o * block_rows).astype(I32)
    local_row = data_row - owner * block_rows
    relative = along // slot_count ^ owner
    hits = (lax.broadcasted_iota(I32, (sta_size, positions), 0) == owner).astype(F32)
    ahead = jnp.dot(hits.astype(BF16), before, preferred_element_type=F32)
    rank = jnp.sum(ahead * hits, axis=0, keepdims=True).astype(I32)
    goes = row == half_way(owner, sta_size) * capacity + rank
    row_tag = column_sum(jnp.where(goes, local_row, 0).astype(F32))
    template_tag = column_sum(jnp.where(goes, relative, 0).astype(F32))

    count = jnp.zeros((positions, 1), I32)
    for t in range(group_size):
        count = jnp.where(spot // slot_count == t, chan_count[t], count)
    copies[3].wait()
    padded[:, :length] = waves[...].astype(F32)
    raw = padded[...]
    listed = (slot < count).astype(F32)
    gain = listed / jnp.sqrt(column_sum(raw * raw) + epsilon)
    ordered = jnp.dot(
        goes.astype(F32).astype(BF16), (raw * gain).astype(BF16), preferred_element_type=F32
    )
    wide = lax.broadcasted_iota(I32, (positions, width), 1)
    sent[...] = jnp.where(
        wide == length, row_tag, jnp.where(wide == length + 1, template_tag, ordered)
    ).astype(BF16)


def prepare_kernel(length, prior, window, shifted, scales, extended):
    rows, before = prior.shape
    lags = window.shape[1]
    total = extended.shape[1]
    start = before // LANE * LANE
    extended[:, :start] = jnp.zeros((rows, start), F32)
    extended[:, start:] = jnp.zeros((rows, total - start), F32)
    extended[:, start : start + lags] = window[...].astype(F32)
    moved = pltpu.roll(extended[:, start:], before - start, axis=1)
    extended[:, start:] = jnp.zeros((rows, total - start), F32)
    extended[:, :before] = prior[...].astype(F32)
    extended[:, start:] = extended[:, start:] + moved
    whole = extended[...]
    used = shifted.shape[1]
    for turn in range(TURNS):
        moved = whole if turn == 0 else pltpu.roll(whole, total - turn * STEP, axis=1)
        shifted[turn * rows : (turn + 1) * rows, :] = moved[:, :used].astype(BF16)
    square = whole * whole
    high = square.astype(BF16)
    low = (square - high.astype(F32)).astype(BF16)
    span = up(length + LANE - 1, LANE)
    sample = lax.broadcasted_iota(I32, (span, LANE), 0)
    lag = lax.broadcasted_iota(I32, (span, LANE), 1)
    band = ((sample >= lag) & (sample < lag + length)).astype(F32).astype(BF16)
    for a in range(lags // LANE):
        at = slice(a * LANE, a * LANE + span)
        energy = jnp.dot(high[:, at], band, preferred_element_type=F32) + jnp.dot(
            low[:, at], band, preferred_element_type=F32
        )
        scale = 1.0 / jnp.sqrt(energy + epsilon)
        scale_high = scale.astype(BF16)
        scales[:rows, a * LANE : (a + 1) * LANE] = scale_high
        scales[rows:, a * LANE : (a + 1) * LANE] = (scale - scale_high.astype(F32)).astype(BF16)


def correlate_kernel(
    length, arrived, shifted, scales, kept, given, frames, waves, traces, toeplitz, sums
):
    positions, width = arrived.shape
    rows = scales.shape[0] // 2
    lags = scales.shape[1]
    half = kept.shape[0]
    blocks = lags // LANE
    waves[...] = arrived[...].astype(F32)
    wanted = waves[:, length : length + 1].astype(I32)
    template = jnp.broadcast_to(waves[:, length + 1 : length + 2].astype(I32), (positions, LANE))

    pairs = wanted.reshape(positions // GROUP, 1, GROUP, 1)
    twice = jnp.concatenate([pairs, pairs], axis=1).reshape(2 * positions, 1)
    place = lax.broadcasted_iota(I32, (2 * positions, 1), 0)
    moved = place // GROUP % 2 + place % GROUP
    every = lax.broadcasted_iota(I32, (2 * positions, TURNS * rows), 1)
    for q in range(2):
        picks = every == (2 * q + moved) % TURNS * rows + twice
        frames[q] = jnp.dot(
            picks.astype(F32).astype(BF16), shifted[...], preferred_element_type=F32
        ).astype(BF16)
    either = lax.broadcasted_iota(I32, (positions, 2 * rows), 1)
    picks = (either == wanted) | (either == wanted + rows)
    picks = picks.astype(F32).astype(BF16)
    waves[:, width - LANE :] = jnp.where(
        lax.broadcasted_iota(I32, (positions, LANE), 1) < length - (width - LANE),
        waves[:, width - LANE :],
        0.0,
    )
    shape = (blocks * GROUP, LANE)
    member = lax.broadcasted_iota(I32, shape, 0) % GROUP
    low_half = member < TURNS
    turn = (lax.broadcasted_iota(I32, shape, 1) // STEP + 2 * TURNS - member) % TURNS

    for g in range(positions // GROUP):
        first = g * GROUP
        copies = toeplitz.at[g % toeplitz.shape[0]]
        for j in range(GROUP):
            wave = jnp.broadcast_to(waves[first + j : first + j + 1, :], (STEP, width))
            copies[j * STEP : (j + 1) * STEP, :] = pltpu.roll(
                wave, 0, axis=1, stride=1, stride_axis=0
            ).astype(BF16)
        at = slice(g * 2 * GROUP, (g + 1) * 2 * GROUP)
        data = [
            frames[q, at, a * LANE : a * LANE + width] for q in range(2) for a in range(blocks)
        ]
        product = lax.dot_general(
            jnp.concatenate(data, axis=0),
            copies[...],
            (((1,), (1,)), ((), ())),
            preferred_element_type=F32,
        )
        if g == 0:
            traces[...] = jnp.dot(picks, scales[...], preferred_element_type=F32)
        product = product.reshape(2, blocks, 2, GROUP, 2 * LANE)
        own = jnp.zeros(shape, F32)
        for step in range(TURNS):
            part = product[step // 2, :, step % 2].reshape(blocks * GROUP, 2 * LANE)
            part = jnp.where(low_half, part[:, :LANE], part[:, LANE:])
            if step > 0:
                part = pltpu.roll(part, step * STEP, axis=1)
            own = jnp.where(turn == step, part, own)
        own = own.reshape(blocks, GROUP, LANE)
        for a in range(blocks):
            at_lag = slice(a * LANE, (a + 1) * LANE)
            traces[first : first + GROUP, at_lag] = traces[first : first + GROUP, at_lag] * own[a]
        if (g + 1) % CHUNK == 0:
            for t in range(2 * half):
                total = jnp.zeros((GROUP, lags), F32) if g + 1 == CHUNK else sums[t]
                for done in range(g + 1 - CHUNK, g + 1):
                    ready = slice(done * GROUP, (done + 1) * GROUP)
                    mine = (template[ready] == t).astype(F32)
                    total = total + traces[ready, :] * jnp.concatenate([mine] * blocks, axis=1)
                sums[t] = total
    stacked = jnp.sum(sums[...], axis=1)
    kept[...] = stacked[:half]
    given[...] = stacked[half:]


def per_device(window, prior, waves, chan_list, chan_count, station_row):
    sta_size = lax.axis_size("sta")
    sta_pos = lax.axis_index("sta").astype(I32).reshape(1)
    group_size, slot_count, length = waves.shape
    positions = group_size * slot_count
    block_rows = prior.shape[0]
    width = up(length + STEP, LANE)
    lags = window.shape[1] * lax.axis_size("tpl")
    vmem = pl.BlockSpec(memory_space=pltpu.VMEM)
    smem = pl.BlockSpec(memory_space=pltpu.SMEM)

    anywhere = pl.BlockSpec(memory_space=pl.ANY)
    sent = pl.pallas_call(
        functools.partial(route_kernel, sta_size, block_rows),
        out_shape=jax.ShapeDtypeStruct((positions, width), BF16),
        in_specs=[smem] + [anywhere] * 4,
        out_specs=vmem,
        scratch_shapes=[
            pltpu.VMEM((positions, length), BF16),
            pltpu.VMEM((group_size, slot_count), I32),
            pltpu.SMEM((group_size,), I32),
            pltpu.VMEM((1, station_row.shape[0]), I32),
            pltpu.VMEM((group_size, LANE), I32),
            pltpu.VMEM((positions, width), F32),
            pltpu.SemaphoreType.DMA((4,)),
        ],
        name="route",
    )(
        sta_pos,
        waves.reshape(positions, length),
        chan_list,
        chan_count,
        station_row.reshape(1, station_row.shape[0]),
    )
    arrived = lax.all_to_all(
        sent.reshape(sta_size, positions // sta_size, width),
        "sta",
        split_axis=0,
        concat_axis=0,
        tiled=True,
        axis_index_groups=[[half_way(i, sta_size) for i in range(sta_size)]],
    ).reshape(positions, width)

    whole_time = lax.all_gather(window, "tpl", axis=1, tiled=True)
    total = up(prior.shape[1] + lags, LANE)
    used = lags - LANE + width
    shifted, scales = pl.pallas_call(
        functools.partial(prepare_kernel, length),
        out_shape=[
            jax.ShapeDtypeStruct((TURNS * block_rows, used), BF16),
            jax.ShapeDtypeStruct((2 * block_rows, lags), BF16),
        ],
        in_specs=[vmem, vmem],
        out_specs=[vmem, vmem],
        scratch_shapes=[pltpu.VMEM((block_rows, total), F32)],
        compiler_params=pltpu.CompilerParams(vmem_limit_bytes=16 * MIB),
        name="prepare",
    )(prior, whole_time)

    half = group_size // 2
    kept, given = pl.pallas_call(
        functools.partial(correlate_kernel, length),
        out_shape=[jax.ShapeDtypeStruct((half, lags), F32)] * 2,
        in_specs=[vmem] * 3,
        out_specs=[vmem] * 2,
        scratch_shapes=[
            pltpu.VMEM((2, 2 * positions, used), BF16),
            pltpu.VMEM((positions, width), F32),
            pltpu.VMEM((positions, lags), F32),
            pltpu.VMEM((positions // GROUP, GROUP * STEP, width), BF16),
            pltpu.VMEM((group_size, GROUP, lags), F32),
        ],
        compiler_params=pltpu.CompilerParams(vmem_limit_bytes=16 * MIB),
        name="correlate",
    )(arrived, shifted, scales)

    distance = sta_size // 2
    while True:
        pairs = [(i, i ^ distance) for i in range(sta_size)]
        kept = kept + lax.ppermute(given, "sta", pairs)
        if distance == 1:
            return kept
        distance //= 2
        kept, given = kept[:distance], kept[distance:]


def solution(mesh):
    in_specs = (
        P("sta", "tpl"),
        P("sta", None),
        P("tpl", "sta", None),
        P("tpl", "sta"),
        P("tpl"),
        P(),
    )
    out_specs = P(("tpl", "sta"), None)
    return jax.shard_map(
        per_device, mesh=mesh, in_specs=in_specs, out_specs=out_specs, check_vma=False
    )
```

```python
import functools

import jax
import jax.numpy as jnp
from jax import lax
from jax.experimental import pallas as pl
from jax.experimental.pallas import tpu as pltpu
from jax.sharding import PartitionSpec as P

epsilon = 1e-06
LANE = 128
STEP = 32
GROUP = 8
CHUNK = 1
TURNS = LANE // STEP
MIB = 1 << 20
F32, BF16, I32 = jnp.float32, jnp.bfloat16, jnp.int32


def up(value, unit):
    return -(-value // unit) * unit


def column_sum(values):
    return jnp.sum(values, axis=1, keepdims=True)


def half_way(place, size):
    return (place + size // 2) % size


def route_kernel(
    sta_size,
    block_rows,
    sta_pos,
    waves_in,
    chan_list_in,
    chan_count_in,
    station_row_in,
    sent,
    waves,
    chan_list,
    chan_count,
    station_row,
    channels,
    padded,
    arrivals,
):
    copies = [
        pltpu.make_async_copy(source, target, arrivals.at[i])
        for i, (source, target) in enumerate(
            (
                (chan_list_in, chan_list),
                (station_row_in, station_row),
                (chan_count_in, chan_count),
                (waves_in, waves),
            )
        )
    ]
    for copy in copies:
        copy.start()
    positions, length = waves.shape
    group_size, slot_count = chan_list.shape
    width = sent.shape[1]
    capacity = positions // sta_size
    padded[:, width - LANE :] = jnp.zeros((positions, LANE), F32)
    channels[...] = jnp.zeros(channels.shape, I32)
    row = lax.broadcasted_iota(I32, (positions, positions), 0)
    lane = lax.broadcasted_iota(I32, (positions, positions), 1)
    before = (row < lane).astype(F32).astype(BF16)
    spot = lax.broadcasted_iota(I32, (positions, 1), 0)
    slot = sta_pos[0] * slot_count + spot % slot_count
    along = lax.broadcasted_iota(I32, (1, positions), 1)
    for copy in copies[:3]:
        copy.wait()

    channels[:, :slot_count] = chan_list[...]
    channel = channels[...]
    station = (channel * 21846) >> 16
    found = jnp.zeros(channel.shape, I32)
    for first in range(0, station_row.shape[1], LANE):
        some = jnp.broadcast_to(station_row[:, first : first + LANE], channel.shape)
        place = jnp.clip(station - first, 0, LANE - 1)
        here = (station >= first) & (station < first + LANE)
        found = jnp.where(here, jnp.take_along_axis(some, place, axis=1), found)
    data_row = 3 * found + channel - 3 * station
    spread = jnp.where(lax.broadcasted_iota(I32, channel.shape, 1) < slot_count, data_row, 0)
    spread = pltpu.roll(spread.astype(F32), 0, axis=1, stride=slot_count, stride_axis=0)
    data_row = jnp.sum(spread, axis=0, keepdims=True).astype(I32)
    owner = jnp.zeros((1, positions), I32)
    for o in range(1, sta_size):
        owner = owner + (data_row >= o * block_rows).astype(I32)
    local_row = data_row - owner * block_rows
    relative = along // slot_count ^ owner
    hits = (lax.broadcasted_iota(I32, (sta_size, positions), 0) == owner).astype(F32)
    ahead = jnp.dot(hits.astype(BF16), before, preferred_element_type=F32)
    rank = jnp.sum(ahead * hits, axis=0, keepdims=True).astype(I32)
    goes = row == half_way(owner, sta_size) * capacity + rank
    row_tag = column_sum(jnp.where(goes, local_row, 0).astype(F32))
    template_tag = column_sum(jnp.where(goes, relative, 0).astype(F32))

    count = jnp.zeros((positions, 1), I32)
    for t in range(group_size):
        count = jnp.where(spot // slot_count == t, chan_count[t], count)
    copies[3].wait()
    padded[:, :length] = waves[...].astype(F32)
    raw = padded[...]
    listed = (slot < count).astype(F32)
    gain = listed / jnp.sqrt(column_sum(raw * raw) + epsilon)
    ordered = jnp.dot(
        goes.astype(F32).astype(BF16), (raw * gain).astype(BF16), preferred_element_type=F32
    )
    wide = lax.broadcasted_iota(I32, (positions, width), 1)
    sent[...] = jnp.where(
        wide == length, row_tag, jnp.where(wide == length + 1, template_tag, ordered)
    ).astype(BF16)


def prepare_kernel(length, turns, tpl_pos, prior, *refs):
    pieces, (shifted, scales, extended) = refs[: len(turns)], refs[len(turns) :]
    rows, before = prior.shape
    piece = pieces[0].shape[1]
    lags = piece * len(turns)
    total = extended.shape[1]
    start = before // LANE * LANE
    extended[:, :start] = jnp.zeros((rows, start), F32)
    extended[:, start:] = jnp.zeros((rows, total - start), F32)
    for turn, part in zip(turns, pieces):
        first = pl.multiple_of(start + (tpl_pos[0] ^ turn) * piece, LANE)
        extended[:, pl.ds(first, piece)] = part[...].astype(F32)
    moved = pltpu.roll(extended[:, start:], before - start, axis=1)
    extended[:, start:] = jnp.zeros((rows, total - start), F32)
    extended[:, :before] = prior[...].astype(F32)
    extended[:, start:] = extended[:, start:] + moved
    whole = extended[...]
    used = shifted.shape[1]
    for turn in range(TURNS):
        moved = whole if turn == 0 else pltpu.roll(whole, total - turn * STEP, axis=1)
        shifted[turn * rows : (turn + 1) * rows, :] = moved[:, :used].astype(BF16)
    square = whole * whole
    high = square.astype(BF16)
    low = (square - high.astype(F32)).astype(BF16)
    over = length % LANE
    sample = lax.broadcasted_iota(I32, (2 * LANE, LANE), 0) % LANE
    lag = lax.broadcasted_iota(I32, (2 * LANE, LANE), 1)
    masks = [sample >= lag, sample < (lag + over) % LANE, sample >= 0]
    masks = jnp.concatenate([mask.astype(F32) for mask in masks], axis=1).astype(BF16)
    spans = [slice(k * LANE, (k + 1) * LANE) for k in range(total // LANE)]
    squares = [jnp.concatenate([high[:, at], low[:, at]], axis=1) for at in spans]
    sums = jnp.dot(jnp.concatenate(squares, axis=0), masks, preferred_element_type=F32)
    sums = sums.reshape(len(spans), rows, 3 * LANE)
    first, last, every = (sums[:, :, at] for at in spans[:3])
    inside = lax.broadcasted_iota(I32, (rows, LANE), 1) < LANE - over
    for a in range(lags // LANE):
        energy = first[a]
        for k in range(a + 1, a + length // LANE):
            energy = energy + every[k]
        end = a + length // LANE
        energy = energy + jnp.where(inside, last[end], every[end] + last[end + 1])
        scale = 1.0 / jnp.sqrt(energy + epsilon)
        scale_high = scale.astype(BF16)
        scales[:rows, spans[a]] = scale_high
        scales[rows:, spans[a]] = (scale - scale_high.astype(F32)).astype(BF16)


def correlate_kernel(
    length, arrived, shifted, scales, kept, given, frames, waves, traces, toeplitz, sums
):
    positions, width = arrived.shape
    rows = scales.shape[0] // 2
    lags = scales.shape[1]
    half = kept.shape[0]
    blocks = lags // LANE
    waves[...] = arrived[...].astype(F32)
    wanted = waves[:, length : length + 1].astype(I32)
    template = jnp.broadcast_to(waves[:, length + 1 : length + 2].astype(I32), (positions, LANE))

    pairs = wanted.reshape(positions // GROUP, 1, GROUP, 1)
    twice = jnp.concatenate([pairs, pairs], axis=1).reshape(2 * positions, 1)
    place = lax.broadcasted_iota(I32, (2 * positions, 1), 0)
    moved = place // GROUP % 2 + place % GROUP
    every = lax.broadcasted_iota(I32, (2 * positions, TURNS * rows), 1)
    for q in range(2):
        picks = every == (2 * q + moved) % TURNS * rows + twice
        frames[q] = jnp.dot(
            picks.astype(F32).astype(BF16), shifted[...], preferred_element_type=F32
        ).astype(BF16)
    either = lax.broadcasted_iota(I32, (positions, 2 * rows), 1)
    picks = (either == wanted) | (either == wanted + rows)
    picks = picks.astype(F32).astype(BF16)
    waves[:, width - LANE :] = jnp.where(
        lax.broadcasted_iota(I32, (positions, LANE), 1) < length - (width - LANE),
        waves[:, width - LANE :],
        0.0,
    )
    shape = (blocks * GROUP, LANE)
    member = lax.broadcasted_iota(I32, shape, 0) % GROUP
    low_half = member < TURNS
    turn = (lax.broadcasted_iota(I32, shape, 1) // STEP + 2 * TURNS - member) % TURNS

    for g in range(positions // GROUP):
        first = g * GROUP
        copies = toeplitz.at[g % toeplitz.shape[0]]
        for j in range(GROUP):
            wave = jnp.broadcast_to(waves[first + j : first + j + 1, :], (STEP, width))
            copies[j * STEP : (j + 1) * STEP, :] = pltpu.roll(
                wave, 0, axis=1, stride=1, stride_axis=0
            ).astype(BF16)
        at = slice(g * 2 * GROUP, (g + 1) * 2 * GROUP)
        data = [
            frames[q, at, a * LANE : a * LANE + width] for q in range(2) for a in range(blocks)
        ]
        product = lax.dot_general(
            jnp.concatenate(data, axis=0),
            copies[...],
            (((1,), (1,)), ((), ())),
            preferred_element_type=F32,
        )
        if g == 0:
            traces[...] = jnp.dot(picks, scales[...], preferred_element_type=F32)
        product = product.reshape(2, blocks, 2, GROUP, 2 * LANE)
        own = jnp.zeros(shape, F32)
        for step in range(TURNS):
            part = product[step // 2, :, step % 2].reshape(blocks * GROUP, 2 * LANE)
            part = jnp.where(low_half, part[:, :LANE], part[:, LANE:])
            if step > 0:
                part = pltpu.roll(part, step * STEP, axis=1)
            own = jnp.where(turn == step, part, own)
        own = own.reshape(blocks, GROUP, LANE)
        for a in range(blocks):
            at_lag = slice(a * LANE, (a + 1) * LANE)
            traces[first : first + GROUP, at_lag] = traces[first : first + GROUP, at_lag] * own[a]
        if (g + 1) % CHUNK == 0:
            for t in range(2 * half):
                total = jnp.zeros((GROUP, lags), F32) if g + 1 == CHUNK else sums[t]
                for done in range(g + 1 - CHUNK, g + 1):
                    ready = slice(done * GROUP, (done + 1) * GROUP)
                    mine = (template[ready] == t).astype(F32)
                    total = total + traces[ready, :] * jnp.concatenate([mine] * blocks, axis=1)
                sums[t] = total
    stacked = jnp.sum(sums[...], axis=1)
    kept[...] = stacked[:half]
    given[...] = stacked[half:]


def per_device(window, prior, waves, chan_list, chan_count, station_row):
    sta_size = lax.axis_size("sta")
    sta_pos = lax.axis_index("sta").astype(I32).reshape(1)
    group_size, slot_count, length = waves.shape
    positions = group_size * slot_count
    block_rows = prior.shape[0]
    width = up(length + STEP, LANE)
    tpl_size = lax.axis_size("tpl")
    lags = window.shape[1] * tpl_size
    vmem = pl.BlockSpec(memory_space=pltpu.VMEM)
    smem = pl.BlockSpec(memory_space=pltpu.SMEM)

    anywhere = pl.BlockSpec(memory_space=pl.ANY)
    sent = pl.pallas_call(
        functools.partial(route_kernel, sta_size, block_rows),
        out_shape=jax.ShapeDtypeStruct((positions, width), BF16),
        in_specs=[smem] + [anywhere] * 4,
        out_specs=vmem,
        scratch_shapes=[
            pltpu.VMEM((positions, length), BF16),
            pltpu.VMEM((group_size, slot_count), I32),
            pltpu.SMEM((group_size,), I32),
            pltpu.VMEM((1, station_row.shape[0]), I32),
            pltpu.VMEM((group_size, LANE), I32),
            pltpu.VMEM((positions, width), F32),
            pltpu.SemaphoreType.DMA((4,)),
        ],
        name="route",
    )(
        sta_pos,
        waves.reshape(positions, length),
        chan_list,
        chan_count,
        station_row.reshape(1, station_row.shape[0]),
    )
    arrived = lax.all_to_all(
        sent.reshape(sta_size, positions // sta_size, width),
        "sta",
        split_axis=0,
        concat_axis=0,
        tiled=True,
        axis_index_groups=[[half_way(i, sta_size) for i in range(sta_size)]],
    ).reshape(positions, width)

    pieces, turns = [window], [0]
    distance = tpl_size // 2
    while distance >= 1:
        hop = distance | 1
        pairs = [(i, i ^ hop) for i in range(tpl_size)]
        pieces = pieces + [lax.ppermute(piece, "tpl", pairs) for piece in pieces]
        turns = turns + [turn ^ hop for turn in turns]
        distance //= 2
    total = up(prior.shape[1] + lags, LANE)
    used = lags - LANE + width
    shifted, scales = pl.pallas_call(
        functools.partial(prepare_kernel, length, turns),
        out_shape=[
            jax.ShapeDtypeStruct((TURNS * block_rows, used), BF16),
            jax.ShapeDtypeStruct((2 * block_rows, lags), BF16),
        ],
        in_specs=[smem] + [vmem] * (1 + tpl_size),
        out_specs=[vmem, vmem],
        scratch_shapes=[pltpu.VMEM((block_rows, total), F32)],
        compiler_params=pltpu.CompilerParams(vmem_limit_bytes=16 * MIB),
        name="prepare",
    )(lax.axis_index("tpl").astype(I32).reshape(1), prior, *pieces)

    half = group_size // 2
    kept, given = pl.pallas_call(
        functools.partial(correlate_kernel, length),
        out_shape=[jax.ShapeDtypeStruct((half, lags), F32)] * 2,
        in_specs=[vmem] * 3,
        out_specs=[vmem] * 2,
        scratch_shapes=[
            pltpu.VMEM((2, 2 * positions, used), BF16),
            pltpu.VMEM((positions, width), F32),
            pltpu.VMEM((positions, lags), F32),
            pltpu.VMEM((positions // GROUP, GROUP * STEP, width), BF16),
            pltpu.VMEM((group_size, GROUP, lags), F32),
        ],
        compiler_params=pltpu.CompilerParams(vmem_limit_bytes=16 * MIB),
        name="correlate",
    )(arrived, shifted, scales)

    distance = sta_size // 2
    while True:
        pairs = [(i, i ^ distance) for i in range(sta_size)]
        kept = kept + lax.ppermute(given, "sta", pairs)
        if distance == 1:
            return kept
        distance //= 2
        kept, given = kept[:distance], kept[distance:]


def solution(mesh):
    in_specs = (
        P("sta", "tpl"),
        P("sta", None),
        P("tpl", "sta", None),
        P("tpl", "sta"),
        P("tpl"),
        P(),
    )
    out_specs = P(("tpl", "sta"), None)
    return jax.shard_map(
        per_device, mesh=mesh, in_specs=in_specs, out_specs=out_specs, check_vma=False
    )
```

```python
import functools

import jax
import jax.numpy as jnp
from jax import lax
from jax.experimental import pallas as pl
from jax.experimental.pallas import tpu as pltpu
from jax.sharding import PartitionSpec as P

epsilon = 1e-06
LANE = 128
STEP = 32
GROUP = 8
CHUNK = 1
TURNS = LANE // STEP
MIB = 1 << 20
F32, BF16, I32 = jnp.float32, jnp.bfloat16, jnp.int32


def up(value, unit):
    return -(-value // unit) * unit


def column_sum(values):
    return jnp.sum(values, axis=1, keepdims=True)


def group_order(size):
    middle = size // 2
    order = []
    for odd in range(2):
        order += range(middle + odd, -1, -2)
        order += range(middle + odd + 2, size, 2)
    return order


def route_kernel(
    sta_size,
    block_rows,
    sta_pos,
    waves_in,
    chan_list_in,
    chan_count_in,
    station_row_in,
    sent,
    waves,
    chan_list,
    chan_count,
    station_row,
    channels,
    padded,
    arrivals,
):
    copies = [
        pltpu.make_async_copy(source, target, arrivals.at[i])
        for i, (source, target) in enumerate(
            (
                (chan_list_in, chan_list),
                (station_row_in, station_row),
                (chan_count_in, chan_count),
                (waves_in, waves),
            )
        )
    ]
    for copy in copies:
        copy.start()
    positions, length = waves.shape
    group_size, slot_count = chan_list.shape
    width = sent.shape[1]
    capacity = positions // sta_size
    padded[:, width - LANE :] = jnp.zeros((positions, LANE), F32)
    channels[...] = jnp.zeros(channels.shape, I32)
    row = lax.broadcasted_iota(I32, (positions, positions), 0)
    lane = lax.broadcasted_iota(I32, (positions, positions), 1)
    before = (row < lane).astype(F32).astype(BF16)
    spot = lax.broadcasted_iota(I32, (positions, 1), 0)
    slot = sta_pos[0] * slot_count + spot % slot_count
    along = lax.broadcasted_iota(I32, (1, positions), 1)
    for copy in copies[:3]:
        copy.wait()

    channels[:, :slot_count] = chan_list[...]
    channel = channels[...]
    station = (channel * 21846) >> 16
    found = jnp.zeros(channel.shape, I32)
    for first in range(0, station_row.shape[1], LANE):
        some = jnp.broadcast_to(station_row[:, first : first + LANE], channel.shape)
        place = jnp.clip(station - first, 0, LANE - 1)
        here = (station >= first) & (station < first + LANE)
        found = jnp.where(here, jnp.take_along_axis(some, place, axis=1), found)
    data_row = 3 * found + channel - 3 * station
    spread = jnp.where(lax.broadcasted_iota(I32, channel.shape, 1) < slot_count, data_row, 0)
    spread = pltpu.roll(spread.astype(F32), 0, axis=1, stride=slot_count, stride_axis=0)
    data_row = jnp.sum(spread, axis=0, keepdims=True).astype(I32)
    owner = jnp.zeros((1, positions), I32)
    for o in range(1, sta_size):
        owner = owner + (data_row >= o * block_rows).astype(I32)
    local_row = data_row - owner * block_rows
    hits = (lax.broadcasted_iota(I32, (sta_size, positions), 0) == owner).astype(F32)
    ahead = jnp.dot(hits.astype(BF16), before, preferred_element_type=F32)
    rank = jnp.sum(ahead * hits, axis=0, keepdims=True).astype(I32)
    place = jnp.zeros((1, positions), I32)
    for k, o in enumerate(group_order(sta_size)):
        place = jnp.where(owner == o, k * capacity, place)
    goes = row == place + rank
    row_tag = column_sum(jnp.where(goes, local_row, 0).astype(F32))
    template_tag = column_sum(jnp.where(goes, along // slot_count, 0).astype(F32))

    count = jnp.zeros((positions, 1), I32)
    for t in range(group_size):
        count = jnp.where(spot // slot_count == t, chan_count[t], count)
    copies[3].wait()
    padded[:, :length] = waves[...].astype(F32)
    raw = padded[...]
    listed = (slot < count).astype(F32)
    gain = listed / jnp.sqrt(column_sum(raw * raw) + epsilon)
    ordered = jnp.dot(
        goes.astype(F32).astype(BF16), (raw * gain).astype(BF16), preferred_element_type=F32
    )
    wide = lax.broadcasted_iota(I32, (positions, width), 1)
    sent[...] = jnp.where(
        wide == length, row_tag, jnp.where(wide == length + 1, template_tag, ordered)
    ).astype(BF16)


def prepare_kernel(length, turns, tpl_pos, prior, *refs):
    pieces, (shifted, scales, extended) = refs[: len(turns)], refs[len(turns) :]
    rows, before = prior.shape
    piece = pieces[0].shape[1]
    lags = piece * len(turns)
    total = extended.shape[1]
    start = before // LANE * LANE
    extended[:, :start] = jnp.zeros((rows, start), F32)
    extended[:, start:] = jnp.zeros((rows, total - start), F32)
    for turn, part in zip(turns, pieces):
        first = pl.multiple_of(start + (tpl_pos[0] ^ turn) * piece, LANE)
        extended[:, pl.ds(first, piece)] = part[...].astype(F32)
    moved = pltpu.roll(extended[:, start:], before - start, axis=1)
    extended[:, start:] = jnp.zeros((rows, total - start), F32)
    extended[:, :before] = prior[...].astype(F32)
    extended[:, start:] = extended[:, start:] + moved
    whole = extended[...]
    used = shifted.shape[1]
    for turn in range(TURNS):
        moved = whole if turn == 0 else pltpu.roll(whole, total - turn * STEP, axis=1)
        shifted[turn * rows : (turn + 1) * rows, :] = moved[:, :used].astype(BF16)
    square = whole * whole
    high = square.astype(BF16)
    low = (square - high.astype(F32)).astype(BF16)
    over = length % LANE
    sample = lax.broadcasted_iota(I32, (2 * LANE, LANE), 0) % LANE
    lag = lax.broadcasted_iota(I32, (2 * LANE, LANE), 1)
    masks = [sample >= lag, sample < (lag + over) % LANE, sample >= 0]
    masks = jnp.concatenate([mask.astype(F32) for mask in masks], axis=1).astype(BF16)
    spans = [slice(k * LANE, (k + 1) * LANE) for k in range(total // LANE)]
    squares = [jnp.concatenate([high[:, at], low[:, at]], axis=1) for at in spans]
    sums = jnp.dot(jnp.concatenate(squares, axis=0), masks, preferred_element_type=F32)
    sums = sums.reshape(len(spans), rows, 3 * LANE)
    first, last, every = (sums[:, :, at] for at in spans[:3])
    inside = lax.broadcasted_iota(I32, (rows, LANE), 1) < LANE - over
    for a in range(lags // LANE):
        energy = first[a]
        for k in range(a + 1, a + length // LANE):
            energy = energy + every[k]
        end = a + length // LANE
        energy = energy + jnp.where(inside, last[end], every[end] + last[end + 1])
        scale = 1.0 / jnp.sqrt(energy + epsilon)
        scale_high = scale.astype(BF16)
        scales[:rows, spans[a]] = scale_high
        scales[rows:, spans[a]] = (scale - scale_high.astype(F32)).astype(BF16)


def correlate_kernel(
    length, order, arrived, shifted, scales, stacked, frames, waves, traces, toeplitz, sums
):
    positions, width = arrived.shape
    rows = scales.shape[0] // 2
    lags = scales.shape[1]
    blocks = lags // LANE
    waves[...] = arrived[...].astype(F32)
    wanted = waves[:, length : length + 1].astype(I32)
    template = jnp.broadcast_to(waves[:, length + 1 : length + 2].astype(I32), (positions, LANE))

    pairs = wanted.reshape(positions // GROUP, 1, GROUP, 1)
    twice = jnp.concatenate([pairs, pairs], axis=1).reshape(2 * positions, 1)
    place = lax.broadcasted_iota(I32, (2 * positions, 1), 0)
    moved = place // GROUP % 2 + place % GROUP
    every = lax.broadcasted_iota(I32, (2 * positions, TURNS * rows), 1)
    for q in range(2):
        picks = every == (2 * q + moved) % TURNS * rows + twice
        frames[q] = jnp.dot(
            picks.astype(F32).astype(BF16), shifted[...], preferred_element_type=F32
        ).astype(BF16)
    either = lax.broadcasted_iota(I32, (positions, 2 * rows), 1)
    picks = (either == wanted) | (either == wanted + rows)
    picks = picks.astype(F32).astype(BF16)
    waves[:, width - LANE :] = jnp.where(
        lax.broadcasted_iota(I32, (positions, LANE), 1) < length - (width - LANE),
        waves[:, width - LANE :],
        0.0,
    )
    shape = (blocks * GROUP, LANE)
    member = lax.broadcasted_iota(I32, shape, 0) % GROUP
    low_half = member < TURNS
    turn = (lax.broadcasted_iota(I32, shape, 1) // STEP + 2 * TURNS - member) % TURNS

    for g in range(positions // GROUP):
        first = g * GROUP
        copies = toeplitz.at[g % toeplitz.shape[0]]
        for j in range(GROUP):
            wave = jnp.broadcast_to(waves[first + j : first + j + 1, :], (STEP, width))
            copies[j * STEP : (j + 1) * STEP, :] = pltpu.roll(
                wave, 0, axis=1, stride=1, stride_axis=0
            ).astype(BF16)
        at = slice(g * 2 * GROUP, (g + 1) * 2 * GROUP)
        data = [
            frames[q, at, a * LANE : a * LANE + width] for q in range(2) for a in range(blocks)
        ]
        product = lax.dot_general(
            jnp.concatenate(data, axis=0),
            copies[...],
            (((1,), (1,)), ((), ())),
            preferred_element_type=F32,
        )
        if g == 0:
            traces[...] = jnp.dot(picks, scales[...], preferred_element_type=F32)
        product = product.reshape(2, blocks, 2, GROUP, 2 * LANE)
        own = jnp.zeros(shape, F32)
        for step in range(TURNS):
            part = product[step // 2, :, step % 2].reshape(blocks * GROUP, 2 * LANE)
            part = jnp.where(low_half, part[:, :LANE], part[:, LANE:])
            if step > 0:
                part = pltpu.roll(part, step * STEP, axis=1)
            own = jnp.where(turn == step, part, own)
        own = own.reshape(blocks, GROUP, LANE)
        for a in range(blocks):
            at_lag = slice(a * LANE, (a + 1) * LANE)
            traces[first : first + GROUP, at_lag] = traces[first : first + GROUP, at_lag] * own[a]
        if (g + 1) % CHUNK == 0:
            for t in range(len(order)):
                total = jnp.zeros((GROUP, lags), F32) if g + 1 == CHUNK else sums[t]
                for done in range(g + 1 - CHUNK, g + 1):
                    ready = slice(done * GROUP, (done + 1) * GROUP)
                    mine = (template[ready] == t).astype(F32)
                    total = total + traces[ready, :] * jnp.concatenate([mine] * blocks, axis=1)
                sums[t] = total
    for k, t in enumerate(order):
        lines = [
            jnp.sum(sums[t, :, a * LANE : (a + 1) * LANE], axis=0, keepdims=True)
            for a in range(blocks)
        ]
        stacked[k] = jnp.concatenate(lines, axis=0)


def per_device(window, prior, waves, chan_list, chan_count, station_row):
    sta_size = lax.axis_size("sta")
    sta_pos = lax.axis_index("sta").astype(I32).reshape(1)
    group_size, slot_count, length = waves.shape
    positions = group_size * slot_count
    block_rows = prior.shape[0]
    width = up(length + STEP, LANE)
    tpl_size = lax.axis_size("tpl")
    lags = window.shape[1] * tpl_size
    order = group_order(sta_size)
    vmem = pl.BlockSpec(memory_space=pltpu.VMEM)
    smem = pl.BlockSpec(memory_space=pltpu.SMEM)

    anywhere = pl.BlockSpec(memory_space=pl.ANY)
    sent = pl.pallas_call(
        functools.partial(route_kernel, sta_size, block_rows),
        out_shape=jax.ShapeDtypeStruct((positions, width), BF16),
        in_specs=[smem] + [anywhere] * 4,
        out_specs=vmem,
        scratch_shapes=[
            pltpu.VMEM((positions, length), BF16),
            pltpu.VMEM((group_size, slot_count), I32),
            pltpu.SMEM((group_size,), I32),
            pltpu.VMEM((1, station_row.shape[0]), I32),
            pltpu.VMEM((group_size, LANE), I32),
            pltpu.VMEM((positions, width), F32),
            pltpu.SemaphoreType.DMA((4,)),
        ],
        name="route",
    )(
        sta_pos,
        waves.reshape(positions, length),
        chan_list,
        chan_count,
        station_row.reshape(1, station_row.shape[0]),
    )
    arrived = lax.all_to_all(
        sent.reshape(sta_size, positions // sta_size, width),
        "sta",
        split_axis=0,
        concat_axis=0,
        tiled=True,
        axis_index_groups=[order],
    ).reshape(positions, width)

    pieces, turns = [window], [0]
    distance = tpl_size // 2
    while distance >= 1:
        hop = distance | 1
        pairs = [(i, i ^ hop) for i in range(tpl_size)]
        pieces = pieces + [lax.ppermute(piece, "tpl", pairs) for piece in pieces]
        turns = turns + [turn ^ hop for turn in turns]
        distance //= 2
    total = up(prior.shape[1] + lags, LANE)
    used = lags - LANE + width
    shifted, scales = pl.pallas_call(
        functools.partial(prepare_kernel, length, turns),
        out_shape=[
            jax.ShapeDtypeStruct((TURNS * block_rows, used), BF16),
            jax.ShapeDtypeStruct((2 * block_rows, lags), BF16),
        ],
        in_specs=[smem] + [vmem] * (1 + tpl_size),
        out_specs=[vmem, vmem],
        scratch_shapes=[pltpu.VMEM((block_rows, total), F32)],
        compiler_params=pltpu.CompilerParams(vmem_limit_bytes=16 * MIB),
        name="prepare",
    )(lax.axis_index("tpl").astype(I32).reshape(1), prior, *pieces)

    each = group_size // sta_size
    templates = [o * each + i for o in order for i in range(each)]
    stacked = pl.pallas_call(
        functools.partial(correlate_kernel, length, templates),
        out_shape=jax.ShapeDtypeStruct((group_size, lags // LANE, LANE), F32),
        in_specs=[vmem] * 3,
        out_specs=vmem,
        scratch_shapes=[
            pltpu.VMEM((2, 2 * positions, used), BF16),
            pltpu.VMEM((positions, width), F32),
            pltpu.VMEM((positions, lags), F32),
            pltpu.VMEM((positions // GROUP, GROUP * STEP, width), BF16),
            pltpu.VMEM((group_size, GROUP, lags), F32),
        ],
        compiler_params=pltpu.CompilerParams(vmem_limit_bytes=16 * MIB),
        name="correlate",
    )(arrived, shifted, scales)
    parts = lax.all_to_all(
        stacked, "sta", split_axis=0, concat_axis=0, tiled=True, axis_index_groups=[order]
    )
    parts = parts.reshape(sta_size, each, lags // LANE, LANE)
    return jnp.sum(parts, axis=0).reshape(each, lags)


def solution(mesh):
    in_specs = (
        P("sta", "tpl"),
        P("sta", None),
        P("tpl", "sta", None),
        P("tpl", "sta"),
        P("tpl"),
        P(),
    )
    out_specs = P(("tpl", "sta"), None)
    return jax.shard_map(
        per_device, mesh=mesh, in_specs=in_specs, out_specs=out_specs, check_vma=False
    )
```

```python
import functools

import jax
import jax.numpy as jnp
from jax import lax
from jax.experimental import pallas as pl
from jax.experimental.pallas import tpu as pltpu
from jax.sharding import PartitionSpec as P

epsilon = 1e-06
LANE = 128
STEP = 32
GROUP = 8
CHUNK = 1
TURNS = LANE // STEP
MIB = 1 << 20
F32, BF16, I32 = jnp.float32, jnp.bfloat16, jnp.int32


def up(value, unit):
    return -(-value // unit) * unit


def column_sum(values):
    return jnp.sum(values, axis=1, keepdims=True)


def waves_order(size):
    return [(i + size // 2 - 1) % size for i in range(size)]


def stacks_order(size):
    middle = size // 2
    order = []
    for odd in range(2):
        order += range(middle + odd, -1, -2)
        order += range(middle + odd + 2, size, 2)
    return order


def route_kernel(
    sta_size,
    block_rows,
    sta_pos,
    waves_in,
    chan_list_in,
    chan_count_in,
    station_row_in,
    sent,
    waves,
    chan_list,
    chan_count,
    station_row,
    channels,
    padded,
    arrivals,
):
    copies = [
        pltpu.make_async_copy(source, target, arrivals.at[i])
        for i, (source, target) in enumerate(
            (
                (chan_list_in, chan_list),
                (station_row_in, station_row),
                (chan_count_in, chan_count),
                (waves_in, waves),
            )
        )
    ]
    for copy in copies:
        copy.start()
    positions, length = waves.shape
    group_size, slot_count = chan_list.shape
    width = sent.shape[1]
    capacity = positions // sta_size
    padded[:, width - LANE :] = jnp.zeros((positions, LANE), F32)
    channels[...] = jnp.zeros(channels.shape, I32)
    row = lax.broadcasted_iota(I32, (positions, positions), 0)
    lane = lax.broadcasted_iota(I32, (positions, positions), 1)
    before = (row < lane).astype(F32).astype(BF16)
    spot = lax.broadcasted_iota(I32, (positions, 1), 0)
    slot = sta_pos[0] * slot_count + spot % slot_count
    along = lax.broadcasted_iota(I32, (1, positions), 1)
    for copy in copies[:3]:
        copy.wait()

    channels[:, :slot_count] = chan_list[...]
    channel = channels[...]
    station = (channel * 21846) >> 16
    found = jnp.zeros(channel.shape, I32)
    for first in range(0, station_row.shape[1], LANE):
        some = jnp.broadcast_to(station_row[:, first : first + LANE], channel.shape)
        place = jnp.clip(station - first, 0, LANE - 1)
        here = (station >= first) & (station < first + LANE)
        found = jnp.where(here, jnp.take_along_axis(some, place, axis=1), found)
    data_row = 3 * found + channel - 3 * station
    spread = jnp.where(lax.broadcasted_iota(I32, channel.shape, 1) < slot_count, data_row, 0)
    spread = pltpu.roll(spread.astype(F32), 0, axis=1, stride=slot_count, stride_axis=0)
    data_row = jnp.sum(spread, axis=0, keepdims=True).astype(I32)
    owner = jnp.zeros((1, positions), I32)
    for o in range(1, sta_size):
        owner = owner + (data_row >= o * block_rows).astype(I32)
    local_row = data_row - owner * block_rows
    hits = (lax.broadcasted_iota(I32, (sta_size, positions), 0) == owner).astype(F32)
    ahead = jnp.dot(hits.astype(BF16), before, preferred_element_type=F32)
    rank = jnp.sum(ahead * hits, axis=0, keepdims=True).astype(I32)
    place = jnp.zeros((1, positions), I32)
    for k, o in enumerate(waves_order(sta_size)):
        place = jnp.where(owner == o, k * capacity, place)
    goes = row == place + rank
    row_tag = column_sum(jnp.where(goes, local_row, 0).astype(F32))
    template_tag = column_sum(jnp.where(goes, along // slot_count, 0).astype(F32))

    count = jnp.zeros((positions, 1), I32)
    for t in range(group_size):
        count = jnp.where(spot // slot_count == t, chan_count[t], count)
    copies[3].wait()
    padded[:, :length] = waves[...].astype(F32)
    raw = padded[...]
    listed = (slot < count).astype(F32)
    gain = listed / jnp.sqrt(column_sum(raw * raw) + epsilon)
    ordered = jnp.dot(
        goes.astype(F32).astype(BF16), (raw * gain).astype(BF16), preferred_element_type=F32
    )
    wide = lax.broadcasted_iota(I32, (positions, width), 1)
    sent[...] = jnp.where(
        wide == length, row_tag, jnp.where(wide == length + 1, template_tag, ordered)
    ).astype(BF16)


def prepare_kernel(length, turns, tpl_pos, prior, *refs):
    pieces, (shifted, scales, extended) = refs[: len(turns)], refs[len(turns) :]
    rows, before = prior.shape
    piece = pieces[0].shape[1]
    lags = piece * len(turns)
    total = extended.shape[1]
    start = before // LANE * LANE
    extended[:, :start] = jnp.zeros((rows, start), F32)
    extended[:, start:] = jnp.zeros((rows, total - start), F32)
    for turn, part in zip(turns, pieces):
        first = pl.multiple_of(start + (tpl_pos[0] ^ turn) * piece, LANE)
        extended[:, pl.ds(first, piece)] = part[...].astype(F32)
    moved = pltpu.roll(extended[:, start:], before - start, axis=1)
    extended[:, start:] = jnp.zeros((rows, total - start), F32)
    extended[:, :before] = prior[...].astype(F32)
    extended[:, start:] = extended[:, start:] + moved
    whole = extended[...]
    used = shifted.shape[1]
    for turn in range(TURNS):
        moved = whole if turn == 0 else pltpu.roll(whole, total - turn * STEP, axis=1)
        shifted[turn * rows : (turn + 1) * rows, :] = moved[:, :used].astype(BF16)
    square = whole * whole
    high = square.astype(BF16)
    low = (square - high.astype(F32)).astype(BF16)
    over = length % LANE
    sample = lax.broadcasted_iota(I32, (2 * LANE, LANE), 0) % LANE
    lag = lax.broadcasted_iota(I32, (2 * LANE, LANE), 1)
    masks = [sample >= lag, sample < (lag + over) % LANE, sample >= 0]
    masks = jnp.concatenate([mask.astype(F32) for mask in masks], axis=1).astype(BF16)
    spans = [slice(k * LANE, (k + 1) * LANE) for k in range(total // LANE)]
    squares = [jnp.concatenate([high[:, at], low[:, at]], axis=1) for at in spans]
    sums = jnp.dot(jnp.concatenate(squares, axis=0), masks, preferred_element_type=F32)
    sums = sums.reshape(len(spans), rows, 3 * LANE)
    first, last, every = (sums[:, :, at] for at in spans[:3])
    inside = lax.broadcasted_iota(I32, (rows, LANE), 1) < LANE - over
    for a in range(lags // LANE):
        energy = first[a]
        for k in range(a + 1, a + length // LANE):
            energy = energy + every[k]
        end = a + length // LANE
        energy = energy + jnp.where(inside, last[end], every[end] + last[end + 1])
        scale = 1.0 / jnp.sqrt(energy + epsilon)
        scale_high = scale.astype(BF16)
        scales[:rows, spans[a]] = scale_high
        scales[rows:, spans[a]] = (scale - scale_high.astype(F32)).astype(BF16)


def correlate_kernel(
    length, order, arrived, shifted, scales, stacked, frames, waves, traces, toeplitz, sums
):
    positions, width = arrived.shape
    rows = scales.shape[0] // 2
    lags = scales.shape[1]
    blocks = lags // LANE
    waves[...] = arrived[...].astype(F32)
    wanted = waves[:, length : length + 1].astype(I32)
    template = jnp.broadcast_to(waves[:, length + 1 : length + 2].astype(I32), (positions, LANE))

    pairs = wanted.reshape(positions // GROUP, 1, GROUP, 1)
    twice = jnp.concatenate([pairs, pairs], axis=1).reshape(2 * positions, 1)
    place = lax.broadcasted_iota(I32, (2 * positions, 1), 0)
    moved = place // GROUP % 2 + place % GROUP
    every = lax.broadcasted_iota(I32, (2 * positions, TURNS * rows), 1)
    for q in range(2):
        picks = every == (2 * q + moved) % TURNS * rows + twice
        frames[q] = jnp.dot(
            picks.astype(F32).astype(BF16), shifted[...], preferred_element_type=F32
        ).astype(BF16)
    either = lax.broadcasted_iota(I32, (positions, 2 * rows), 1)
    picks = (either == wanted) | (either == wanted + rows)
    picks = picks.astype(F32).astype(BF16)
    waves[:, width - LANE :] = jnp.where(
        lax.broadcasted_iota(I32, (positions, LANE), 1) < length - (width - LANE),
        waves[:, width - LANE :],
        0.0,
    )
    shape = (blocks * GROUP, LANE)
    member = lax.broadcasted_iota(I32, shape, 0) % GROUP
    low_half = member < TURNS
    turn = (lax.broadcasted_iota(I32, shape, 1) // STEP + 2 * TURNS - member) % TURNS

    for g in range(positions // GROUP):
        first = g * GROUP
        copies = toeplitz.at[g % toeplitz.shape[0]]
        for j in range(GROUP):
            wave = jnp.broadcast_to(waves[first + j : first + j + 1, :], (STEP, width))
            copies[j * STEP : (j + 1) * STEP, :] = pltpu.roll(
                wave, 0, axis=1, stride=1, stride_axis=0
            ).astype(BF16)
        at = slice(g * 2 * GROUP, (g + 1) * 2 * GROUP)
        data = [
            frames[q, at, a * LANE : a * LANE + width] for q in range(2) for a in range(blocks)
        ]
        product = lax.dot_general(
            jnp.concatenate(data, axis=0),
            copies[...],
            (((1,), (1,)), ((), ())),
            preferred_element_type=F32,
        )
        if g == 0:
            traces[...] = jnp.dot(picks, scales[...], preferred_element_type=F32)
        product = product.reshape(2, blocks, 2, GROUP, 2 * LANE)
        own = jnp.zeros(shape, F32)
        for step in range(TURNS):
            part = product[step // 2, :, step % 2].reshape(blocks * GROUP, 2 * LANE)
            part = jnp.where(low_half, part[:, :LANE], part[:, LANE:])
            if step > 0:
                part = pltpu.roll(part, step * STEP, axis=1)
            own = jnp.where(turn == step, part, own)
        own = own.reshape(blocks, GROUP, LANE)
        for a in range(blocks):
            at_lag = slice(a * LANE, (a + 1) * LANE)
            traces[first : first + GROUP, at_lag] = traces[first : first + GROUP, at_lag] * own[a]
        if (g + 1) % CHUNK == 0:
            for t in range(len(order)):
                total = jnp.zeros((GROUP, lags), F32) if g + 1 == CHUNK else sums[t]
                for done in range(g + 1 - CHUNK, g + 1):
                    ready = slice(done * GROUP, (done + 1) * GROUP)
                    mine = (template[ready] == t).astype(F32)
                    total = total + traces[ready, :] * jnp.concatenate([mine] * blocks, axis=1)
                sums[t] = total
    for k, t in enumerate(order):
        lines = [
            jnp.sum(sums[t, :, a * LANE : (a + 1) * LANE], axis=0, keepdims=True)
            for a in range(blocks)
        ]
        stacked[k] = jnp.concatenate(lines, axis=0)


def per_device(window, prior, waves, chan_list, chan_count, station_row):
    sta_size = lax.axis_size("sta")
    sta_pos = lax.axis_index("sta").astype(I32).reshape(1)
    group_size, slot_count, length = waves.shape
    positions = group_size * slot_count
    block_rows = prior.shape[0]
    width = up(length + STEP, LANE)
    tpl_size = lax.axis_size("tpl")
    lags = window.shape[1] * tpl_size
    order = stacks_order(sta_size)
    vmem = pl.BlockSpec(memory_space=pltpu.VMEM)
    smem = pl.BlockSpec(memory_space=pltpu.SMEM)

    anywhere = pl.BlockSpec(memory_space=pl.ANY)
    sent = pl.pallas_call(
        functools.partial(route_kernel, sta_size, block_rows),
        out_shape=jax.ShapeDtypeStruct((positions, width), BF16),
        in_specs=[smem] + [anywhere] * 4,
        out_specs=vmem,
        scratch_shapes=[
            pltpu.VMEM((positions, length), BF16),
            pltpu.VMEM((group_size, slot_count), I32),
            pltpu.SMEM((group_size,), I32),
            pltpu.VMEM((1, station_row.shape[0]), I32),
            pltpu.VMEM((group_size, LANE), I32),
            pltpu.VMEM((positions, width), F32),
            pltpu.SemaphoreType.DMA((4,)),
        ],
        name="route",
    )(
        sta_pos,
        waves.reshape(positions, length),
        chan_list,
        chan_count,
        station_row.reshape(1, station_row.shape[0]),
    )
    arrived = lax.all_to_all(
        sent.reshape(sta_size, positions // sta_size, width),
        "sta",
        split_axis=0,
        concat_axis=0,
        tiled=True,
        axis_index_groups=[waves_order(sta_size)],
    ).reshape(positions, width)

    pieces, turns = [window], [0]
    distance = tpl_size // 2
    while distance >= 1:
        hop = distance | 1
        pairs = [(i, i ^ hop) for i in range(tpl_size)]
        pieces = pieces + [lax.ppermute(piece, "tpl", pairs) for piece in pieces]
        turns = turns + [turn ^ hop for turn in turns]
        distance //= 2
    total = up(prior.shape[1] + lags, LANE)
    used = lags - LANE + width
    shifted, scales = pl.pallas_call(
        functools.partial(prepare_kernel, length, turns),
        out_shape=[
            jax.ShapeDtypeStruct((TURNS * block_rows, used), BF16),
            jax.ShapeDtypeStruct((2 * block_rows, lags), BF16),
        ],
        in_specs=[smem] + [vmem] * (1 + tpl_size),
        out_specs=[vmem, vmem],
        scratch_shapes=[pltpu.VMEM((block_rows, total), F32)],
        compiler_params=pltpu.CompilerParams(vmem_limit_bytes=16 * MIB),
        name="prepare",
    )(lax.axis_index("tpl").astype(I32).reshape(1), prior, *pieces)

    each = group_size // sta_size
    templates = [o * each + i for o in order for i in range(each)]
    stacked = pl.pallas_call(
        functools.partial(correlate_kernel, length, templates),
        out_shape=jax.ShapeDtypeStruct((group_size, lags // LANE, LANE), F32),
        in_specs=[vmem] * 3,
        out_specs=vmem,
        scratch_shapes=[
            pltpu.VMEM((2, 2 * positions, used), BF16),
            pltpu.VMEM((positions, width), F32),
            pltpu.VMEM((positions, lags), F32),
            pltpu.VMEM((positions // GROUP, GROUP * STEP, width), BF16),
            pltpu.VMEM((group_size, GROUP, lags), F32),
        ],
        compiler_params=pltpu.CompilerParams(vmem_limit_bytes=16 * MIB),
        name="correlate",
    )(arrived, shifted, scales)
    parts = lax.all_to_all(
        stacked, "sta", split_axis=0, concat_axis=0, tiled=True, axis_index_groups=[order]
    )
    parts = parts.reshape(sta_size, each, lags // LANE, LANE)
    return jnp.sum(parts, axis=0).reshape(each, lags)


def solution(mesh):
    in_specs = (
        P("sta", "tpl"),
        P("sta", None),
        P("tpl", "sta", None),
        P("tpl", "sta"),
        P("tpl"),
        P(),
    )
    out_specs = P(("tpl", "sta"), None)
    return jax.shard_map(
        per_device, mesh=mesh, in_specs=in_specs, out_specs=out_specs, check_vma=False
    )
```

```python
import functools

import jax
import jax.numpy as jnp
from jax import lax
from jax.experimental import pallas as pl
from jax.experimental.pallas import tpu as pltpu
from jax.sharding import PartitionSpec as P

epsilon = 1e-06
LANE = 128
STEP = 32
GROUP = 8
CHUNK = 1
TURNS = LANE // STEP
MIB = 1 << 20
F32, BF16, I32 = jnp.float32, jnp.bfloat16, jnp.int32


def up(value, unit):
    return -(-value // unit) * unit


def column_sum(values):
    return jnp.sum(values, axis=1, keepdims=True)


def waves_order(size):
    if size == 8:
        return [3, 0, 1, 4, 5, 7, 2, 6]
    return [(i + size // 2 - 1) % size for i in range(size)]


def stacks_order(size):
    middle = size // 2
    order = []
    for odd in range(2):
        order += range(middle + odd, -1, -2)
        order += range(middle + odd + 2, size, 2)
    return order


def route_kernel(
    sta_size,
    block_rows,
    sta_pos,
    waves_in,
    chan_list_in,
    chan_count_in,
    station_row_in,
    sent,
    waves,
    chan_list,
    chan_count,
    station_row,
    channels,
    padded,
    arrivals,
):
    copies = [
        pltpu.make_async_copy(source, target, arrivals.at[i])
        for i, (source, target) in enumerate(
            (
                (chan_list_in, chan_list),
                (station_row_in, station_row),
                (chan_count_in, chan_count),
                (waves_in, waves),
            )
        )
    ]
    for copy in copies:
        copy.start()
    positions, length = waves.shape
    group_size, slot_count = chan_list.shape
    width = sent.shape[1]
    capacity = positions // sta_size
    padded[:, width - LANE :] = jnp.zeros((positions, LANE), F32)
    channels[...] = jnp.zeros(channels.shape, I32)
    row = lax.broadcasted_iota(I32, (positions, positions), 0)
    lane = lax.broadcasted_iota(I32, (positions, positions), 1)
    before = (row < lane).astype(F32).astype(BF16)
    spot = lax.broadcasted_iota(I32, (positions, 1), 0)
    slot = sta_pos[0] * slot_count + spot % slot_count
    along = lax.broadcasted_iota(I32, (1, positions), 1)
    for copy in copies[:3]:
        copy.wait()

    channels[:, :slot_count] = chan_list[...]
    channel = channels[...]
    station = (channel * 21846) >> 16
    found = jnp.zeros(channel.shape, I32)
    for first in range(0, station_row.shape[1], LANE):
        some = jnp.broadcast_to(station_row[:, first : first + LANE], channel.shape)
        place = jnp.clip(station - first, 0, LANE - 1)
        here = (station >= first) & (station < first + LANE)
        found = jnp.where(here, jnp.take_along_axis(some, place, axis=1), found)
    data_row = 3 * found + channel - 3 * station
    spread = jnp.where(lax.broadcasted_iota(I32, channel.shape, 1) < slot_count, data_row, 0)
    spread = pltpu.roll(spread.astype(F32), 0, axis=1, stride=slot_count, stride_axis=0)
    data_row = jnp.sum(spread, axis=0, keepdims=True).astype(I32)
    owner = jnp.zeros((1, positions), I32)
    for o in range(1, sta_size):
        owner = owner + (data_row >= o * block_rows).astype(I32)
    local_row = data_row - owner * block_rows
    hits = (lax.broadcasted_iota(I32, (sta_size, positions), 0) == owner).astype(F32)
    ahead = jnp.dot(hits.astype(BF16), before, preferred_element_type=F32)
    rank = jnp.sum(ahead * hits, axis=0, keepdims=True).astype(I32)
    place = jnp.zeros((1, positions), I32)
    for k, o in enumerate(waves_order(sta_size)):
        place = jnp.where(owner == o, k * capacity, place)
    goes = row == place + rank
    row_tag = column_sum(jnp.where(goes, local_row, 0).astype(F32))
    template_tag = column_sum(jnp.where(goes, along // slot_count, 0).astype(F32))

    count = jnp.zeros((positions, 1), I32)
    for t in range(group_size):
        count = jnp.where(spot // slot_count == t, chan_count[t], count)
    copies[3].wait()
    padded[:, :length] = waves[...].astype(F32)
    raw = padded[...]
    listed = (slot < count).astype(F32)
    gain = listed / jnp.sqrt(column_sum(raw * raw) + epsilon)
    ordered = jnp.dot(
        goes.astype(F32).astype(BF16), (raw * gain).astype(BF16), preferred_element_type=F32
    )
    wide = lax.broadcasted_iota(I32, (positions, width), 1)
    sent[...] = jnp.where(
        wide == length, row_tag, jnp.where(wide == length + 1, template_tag, ordered)
    ).astype(BF16)


def prepare_kernel(length, turns, tpl_pos, prior, *refs):
    pieces, (shifted, scales, extended) = refs[: len(turns)], refs[len(turns) :]
    rows, before = prior.shape
    piece = pieces[0].shape[1]
    lags = piece * len(turns)
    total = extended.shape[1]
    start = before // LANE * LANE
    extended[:, :start] = jnp.zeros((rows, start), F32)
    extended[:, start:] = jnp.zeros((rows, total - start), F32)
    for turn, part in zip(turns, pieces):
        first = pl.multiple_of(start + (tpl_pos[0] ^ turn) * piece, LANE)
        extended[:, pl.ds(first, piece)] = part[...].astype(F32)
    moved = pltpu.roll(extended[:, start:], before - start, axis=1)
    extended[:, start:] = jnp.zeros((rows, total - start), F32)
    extended[:, :before] = prior[...].astype(F32)
    extended[:, start:] = extended[:, start:] + moved
    whole = extended[...]
    used = shifted.shape[1]
    for turn in range(TURNS):
        moved = whole if turn == 0 else pltpu.roll(whole, total - turn * STEP, axis=1)
        shifted[turn * rows : (turn + 1) * rows, :] = moved[:, :used].astype(BF16)
    square = whole * whole
    high = square.astype(BF16)
    low = (square - high.astype(F32)).astype(BF16)
    over = length % LANE
    sample = lax.broadcasted_iota(I32, (2 * LANE, LANE), 0) % LANE
    lag = lax.broadcasted_iota(I32, (2 * LANE, LANE), 1)
    masks = [sample >= lag, sample < (lag + over) % LANE, sample >= 0]
    masks = jnp.concatenate([mask.astype(F32) for mask in masks], axis=1).astype(BF16)
    spans = [slice(k * LANE, (k + 1) * LANE) for k in range(total // LANE)]
    squares = [jnp.concatenate([high[:, at], low[:, at]], axis=1) for at in spans]
    sums = jnp.dot(jnp.concatenate(squares, axis=0), masks, preferred_element_type=F32)
    sums = sums.reshape(len(spans), rows, 3 * LANE)
    first, last, every = (sums[:, :, at] for at in spans[:3])
    inside = lax.broadcasted_iota(I32, (rows, LANE), 1) < LANE - over
    for a in range(lags // LANE):
        energy = first[a]
        for k in range(a + 1, a + length // LANE):
            energy = energy + every[k]
        end = a + length // LANE
        energy = energy + jnp.where(inside, last[end], every[end] + last[end + 1])
        scale = 1.0 / jnp.sqrt(energy + epsilon)
        scale_high = scale.astype(BF16)
        scales[:rows, spans[a]] = scale_high
        scales[rows:, spans[a]] = (scale - scale_high.astype(F32)).astype(BF16)


def correlate_kernel(
    length, order, arrived, shifted, scales, stacked, frames, waves, traces, toeplitz, sums
):
    positions, width = arrived.shape
    rows = scales.shape[0] // 2
    lags = scales.shape[1]
    blocks = lags // LANE
    waves[...] = arrived[...].astype(F32)
    wanted = waves[:, length : length + 1].astype(I32)
    template = jnp.broadcast_to(waves[:, length + 1 : length + 2].astype(I32), (positions, LANE))

    pairs = wanted.reshape(positions // GROUP, 1, GROUP, 1)
    twice = jnp.concatenate([pairs, pairs], axis=1).reshape(2 * positions, 1)
    place = lax.broadcasted_iota(I32, (2 * positions, 1), 0)
    moved = place // GROUP % 2 + place % GROUP
    every = lax.broadcasted_iota(I32, (2 * positions, TURNS * rows), 1)
    for q in range(2):
        picks = every == (2 * q + moved) % TURNS * rows + twice
        frames[q] = jnp.dot(
            picks.astype(F32).astype(BF16), shifted[...], preferred_element_type=F32
        ).astype(BF16)
    either = lax.broadcasted_iota(I32, (positions, 2 * rows), 1)
    picks = (either == wanted) | (either == wanted + rows)
    picks = picks.astype(F32).astype(BF16)
    waves[:, width - LANE :] = jnp.where(
        lax.broadcasted_iota(I32, (positions, LANE), 1) < length - (width - LANE),
        waves[:, width - LANE :],
        0.0,
    )
    shape = (blocks * GROUP, LANE)
    member = lax.broadcasted_iota(I32, shape, 0) % GROUP
    low_half = member < TURNS
    turn = (lax.broadcasted_iota(I32, shape, 1) // STEP + 2 * TURNS - member) % TURNS

    for g in range(positions // GROUP):
        first = g * GROUP
        copies = toeplitz.at[g % toeplitz.shape[0]]
        for j in range(GROUP):
            wave = jnp.broadcast_to(waves[first + j : first + j + 1, :], (STEP, width))
            copies[j * STEP : (j + 1) * STEP, :] = pltpu.roll(
                wave, 0, axis=1, stride=1, stride_axis=0
            ).astype(BF16)
        at = slice(g * 2 * GROUP, (g + 1) * 2 * GROUP)
        data = [
            frames[q, at, a * LANE : a * LANE + width] for q in range(2) for a in range(blocks)
        ]
        product = lax.dot_general(
            jnp.concatenate(data, axis=0),
            copies[...],
            (((1,), (1,)), ((), ())),
            preferred_element_type=F32,
        )
        if g == 0:
            traces[...] = jnp.dot(picks, scales[...], preferred_element_type=F32)
        product = product.reshape(2, blocks, 2, GROUP, 2 * LANE)
        own = jnp.zeros(shape, F32)
        for step in range(TURNS):
            part = product[step // 2, :, step % 2].reshape(blocks * GROUP, 2 * LANE)
            part = jnp.where(low_half, part[:, :LANE], part[:, LANE:])
            if step > 0:
                part = pltpu.roll(part, step * STEP, axis=1)
            own = jnp.where(turn == step, part, own)
        own = own.reshape(blocks, GROUP, LANE)
        for a in range(blocks):
            at_lag = slice(a * LANE, (a + 1) * LANE)
            traces[first : first + GROUP, at_lag] = traces[first : first + GROUP, at_lag] * own[a]
        if (g + 1) % CHUNK == 0:
            for t in range(len(order)):
                total = jnp.zeros((GROUP, lags), F32) if g + 1 == CHUNK else sums[t]
                for done in range(g + 1 - CHUNK, g + 1):
                    ready = slice(done * GROUP, (done + 1) * GROUP)
                    mine = (template[ready] == t).astype(F32)
                    total = total + traces[ready, :] * jnp.concatenate([mine] * blocks, axis=1)
                sums[t] = total
    for k, t in enumerate(order):
        lines = [
            jnp.sum(sums[t, :, a * LANE : (a + 1) * LANE], axis=0, keepdims=True)
            for a in range(blocks)
        ]
        stacked[k] = jnp.concatenate(lines, axis=0)


def per_device(window, prior, waves, chan_list, chan_count, station_row):
    sta_size = lax.axis_size("sta")
    sta_pos = lax.axis_index("sta").astype(I32).reshape(1)
    group_size, slot_count, length = waves.shape
    positions = group_size * slot_count
    block_rows = prior.shape[0]
    width = up(length + STEP, LANE)
    tpl_size = lax.axis_size("tpl")
    lags = window.shape[1] * tpl_size
    order = stacks_order(sta_size)
    vmem = pl.BlockSpec(memory_space=pltpu.VMEM)
    smem = pl.BlockSpec(memory_space=pltpu.SMEM)

    anywhere = pl.BlockSpec(memory_space=pl.ANY)
    sent = pl.pallas_call(
        functools.partial(route_kernel, sta_size, block_rows),
        out_shape=jax.ShapeDtypeStruct((positions, width), BF16),
        in_specs=[smem] + [anywhere] * 4,
        out_specs=vmem,
        scratch_shapes=[
            pltpu.VMEM((positions, length), BF16),
            pltpu.VMEM((group_size, slot_count), I32),
            pltpu.SMEM((group_size,), I32),
            pltpu.VMEM((1, station_row.shape[0]), I32),
            pltpu.VMEM((group_size, LANE), I32),
            pltpu.VMEM((positions, width), F32),
            pltpu.SemaphoreType.DMA((4,)),
        ],
        name="route",
    )(
        sta_pos,
        waves.reshape(positions, length),
        chan_list,
        chan_count,
        station_row.reshape(1, station_row.shape[0]),
    )
    arrived = lax.all_to_all(
        sent.reshape(sta_size, positions // sta_size, width),
        "sta",
        split_axis=0,
        concat_axis=0,
        tiled=True,
        axis_index_groups=[waves_order(sta_size)],
    ).reshape(positions, width)

    pieces, turns = [window], [0]
    distance = tpl_size // 2
    while distance >= 1:
        hop = distance | 1
        pairs = [(i, i ^ hop) for i in range(tpl_size)]
        pieces = pieces + [lax.ppermute(piece, "tpl", pairs) for piece in pieces]
        turns = turns + [turn ^ hop for turn in turns]
        distance //= 2
    total = up(prior.shape[1] + lags, LANE)
    used = lags - LANE + width
    shifted, scales = pl.pallas_call(
        functools.partial(prepare_kernel, length, turns),
        out_shape=[
            jax.ShapeDtypeStruct((TURNS * block_rows, used), BF16),
            jax.ShapeDtypeStruct((2 * block_rows, lags), BF16),
        ],
        in_specs=[smem] + [vmem] * (1 + tpl_size),
        out_specs=[vmem, vmem],
        scratch_shapes=[pltpu.VMEM((block_rows, total), F32)],
        compiler_params=pltpu.CompilerParams(vmem_limit_bytes=16 * MIB),
        name="prepare",
    )(lax.axis_index("tpl").astype(I32).reshape(1), prior, *pieces)

    each = group_size // sta_size
    templates = [o * each + i for o in order for i in range(each)]
    stacked = pl.pallas_call(
        functools.partial(correlate_kernel, length, templates),
        out_shape=jax.ShapeDtypeStruct((group_size, lags // LANE, LANE), F32),
        in_specs=[vmem] * 3,
        out_specs=vmem,
        scratch_shapes=[
            pltpu.VMEM((2, 2 * positions, used), BF16),
            pltpu.VMEM((positions, width), F32),
            pltpu.VMEM((positions, lags), F32),
            pltpu.VMEM((positions // GROUP, GROUP * STEP, width), BF16),
            pltpu.VMEM((group_size, GROUP, lags), F32),
        ],
        compiler_params=pltpu.CompilerParams(vmem_limit_bytes=16 * MIB),
        name="correlate",
    )(arrived, shifted, scales)
    parts = lax.all_to_all(
        stacked, "sta", split_axis=0, concat_axis=0, tiled=True, axis_index_groups=[order]
    )
    parts = parts.reshape(sta_size, each, lags // LANE, LANE)
    return jnp.sum(parts, axis=0).reshape(each, lags)


def solution(mesh):
    in_specs = (
        P("sta", "tpl"),
        P("sta", None),
        P("tpl", "sta", None),
        P("tpl", "sta"),
        P("tpl"),
        P(),
    )
    out_specs = P(("tpl", "sta"), None)
    return jax.shard_map(
        per_device, mesh=mesh, in_specs=in_specs, out_specs=out_specs, check_vma=False
    )
```

```python
import functools

import jax
import jax.numpy as jnp
from jax import lax
from jax.experimental import pallas as pl
from jax.experimental.pallas import tpu as pltpu
from jax.sharding import PartitionSpec as P

epsilon = 1e-06
LANE = 128
STEP = 32
GROUP = 8
CHUNK = 1
TURNS = LANE // STEP
MIB = 1 << 20
F32, BF16, I32 = jnp.float32, jnp.bfloat16, jnp.int32


def up(value, unit):
    return -(-value // unit) * unit


def column_sum(values):
    return jnp.sum(values, axis=1, keepdims=True)


def waves_order(size):
    if size == 8:
        return [3, 0, 1, 4, 5, 7, 2, 6]
    return [(i + size // 2 - 1) % size for i in range(size)]


def stacks_order(size):
    middle = size // 2
    order = []
    for odd in range(2):
        order += range(middle + odd, -1, -2)
        order += range(middle + odd + 2, size, 2)
    return order


def route_kernel(
    sta_size,
    block_rows,
    sta_pos,
    waves_in,
    chan_list_in,
    chan_count_in,
    station_row_in,
    sent,
    waves,
    chan_list,
    chan_count,
    station_row,
    channels,
    padded,
    arrivals,
):
    copies = [
        pltpu.make_async_copy(source, target, arrivals.at[i])
        for i, (source, target) in enumerate(
            (
                (chan_list_in, chan_list),
                (station_row_in, station_row),
                (chan_count_in, chan_count),
                (waves_in, waves),
            )
        )
    ]
    for copy in copies:
        copy.start()
    positions, length = waves.shape
    group_size, slot_count = chan_list.shape
    width = sent.shape[1]
    capacity = positions // sta_size
    padded[:, width - LANE :] = jnp.zeros((positions, LANE), F32)
    channels[...] = jnp.zeros(channels.shape, I32)
    row = lax.broadcasted_iota(I32, (positions, positions), 0)
    lane = lax.broadcasted_iota(I32, (positions, positions), 1)
    before = (row < lane).astype(F32).astype(BF16)
    spot = lax.broadcasted_iota(I32, (positions, 1), 0)
    slot = sta_pos[0] * slot_count + spot % slot_count
    along = lax.broadcasted_iota(I32, (1, positions), 1)
    for copy in copies[:3]:
        copy.wait()

    channels[:, :slot_count] = chan_list[...]
    channel = channels[...]
    station = (channel * 21846) >> 16
    found = jnp.zeros(channel.shape, I32)
    for first in range(0, station_row.shape[1], LANE):
        some = jnp.broadcast_to(station_row[:, first : first + LANE], channel.shape)
        place = jnp.clip(station - first, 0, LANE - 1)
        here = (station >= first) & (station < first + LANE)
        found = jnp.where(here, jnp.take_along_axis(some, place, axis=1), found)
    data_row = 3 * found + channel - 3 * station
    spread = jnp.where(lax.broadcasted_iota(I32, channel.shape, 1) < slot_count, data_row, 0)
    spread = pltpu.roll(spread.astype(F32), 0, axis=1, stride=slot_count, stride_axis=0)
    data_row = jnp.sum(spread, axis=0, keepdims=True).astype(I32)
    owner = jnp.zeros((1, positions), I32)
    for o in range(1, sta_size):
        owner = owner + (data_row >= o * block_rows).astype(I32)
    local_row = data_row - owner * block_rows
    hits = (lax.broadcasted_iota(I32, (sta_size, positions), 0) == owner).astype(F32)
    ahead = jnp.dot(hits.astype(BF16), before, preferred_element_type=F32)
    rank = jnp.sum(ahead * hits, axis=0, keepdims=True).astype(I32)
    place = jnp.zeros((1, positions), I32)
    for k, o in enumerate(waves_order(sta_size)):
        place = jnp.where(owner == o, k * capacity, place)
    goes = row == place + rank
    row_tag = column_sum(jnp.where(goes, local_row, 0).astype(F32))
    template_tag = column_sum(jnp.where(goes, along // slot_count, 0).astype(F32))

    count = jnp.zeros((positions, 1), I32)
    for t in range(group_size):
        count = jnp.where(spot // slot_count == t, chan_count[t], count)
    copies[3].wait()
    padded[:, :length] = waves[...].astype(F32)
    raw = padded[...]
    listed = (slot < count).astype(F32)
    gain = listed / jnp.sqrt(column_sum(raw * raw) + epsilon)
    ordered = jnp.dot(
        goes.astype(F32).astype(BF16), (raw * gain).astype(BF16), preferred_element_type=F32
    )
    wide = lax.broadcasted_iota(I32, (positions, width), 1)
    sent[...] = jnp.where(
        wide == length, row_tag, jnp.where(wide == length + 1, template_tag, ordered)
    ).astype(BF16)


def prepare_kernel(length, turns, tpl_pos, prior, *refs):
    pieces, (shifted, scales, extended) = refs[: len(turns)], refs[len(turns) :]
    rows, before = prior.shape
    piece = pieces[0].shape[1]
    lags = piece * len(turns)
    total = extended.shape[1]
    start = before // LANE * LANE
    extended[:, :start] = jnp.zeros((rows, start), F32)
    extended[:, start:] = jnp.zeros((rows, total - start), F32)
    for turn, part in zip(turns, pieces):
        first = pl.multiple_of(start + (tpl_pos[0] ^ turn) * piece, LANE)
        extended[:, pl.ds(first, piece)] = part[...].astype(F32)
    moved = pltpu.roll(extended[:, start:], before - start, axis=1)
    extended[:, start:] = jnp.zeros((rows, total - start), F32)
    extended[:, :before] = prior[...].astype(F32)
    extended[:, start:] = extended[:, start:] + moved
    whole = extended[...]
    used = shifted.shape[1]
    for turn in range(TURNS):
        moved = whole if turn == 0 else pltpu.roll(whole, total - turn * STEP, axis=1)
        shifted[turn * rows : (turn + 1) * rows, :] = moved[:, :used].astype(BF16)
    square = whole * whole
    high = square.astype(BF16)
    low = (square - high.astype(F32)).astype(BF16)
    over = length % LANE
    sample = lax.broadcasted_iota(I32, (2 * LANE, LANE), 0) % LANE
    lag = lax.broadcasted_iota(I32, (2 * LANE, LANE), 1)
    masks = [sample >= lag, sample < (lag + over) % LANE, sample >= 0]
    masks = jnp.concatenate([mask.astype(F32) for mask in masks], axis=1).astype(BF16)
    spans = [slice(k * LANE, (k + 1) * LANE) for k in range(total // LANE)]
    squares = [jnp.concatenate([high[:, at], low[:, at]], axis=1) for at in spans]
    sums = jnp.dot(jnp.concatenate(squares, axis=0), masks, preferred_element_type=F32)
    sums = sums.reshape(len(spans), rows, 3 * LANE)
    first, last, every = (sums[:, :, at] for at in spans[:3])
    inside = lax.broadcasted_iota(I32, (rows, LANE), 1) < LANE - over
    for a in range(lags // LANE):
        energy = first[a]
        for k in range(a + 1, a + length // LANE):
            energy = energy + every[k]
        end = a + length // LANE
        energy = energy + jnp.where(inside, last[end], every[end] + last[end + 1])
        scale = 1.0 / jnp.sqrt(energy + epsilon)
        scale_high = scale.astype(BF16)
        scales[:rows, spans[a]] = scale_high
        scales[rows:, spans[a]] = (scale - scale_high.astype(F32)).astype(BF16)


def add_rows(tiles):
    size = len(tiles)
    row = lax.broadcasted_iota(I32, tiles[0].shape, 0)
    step = size // 2
    while step >= 1:
        tiles = [
            jnp.where(
                row & step == 0,
                low + pltpu.roll(low, size - step, axis=0),
                high + pltpu.roll(high, step, axis=0),
            )
            for low, high in zip(tiles[:step], tiles[step:])
        ]
        step //= 2
    return tiles[0]


def correlate_kernel(
    length, order, arrived, shifted, scales, stacked, frames, waves, traces, toeplitz, sums
):
    positions, width = arrived.shape
    rows = scales.shape[0] // 2
    lags = scales.shape[1]
    blocks = lags // LANE
    waves[...] = arrived[...].astype(F32)
    wanted = waves[:, length : length + 1].astype(I32)
    template = jnp.broadcast_to(waves[:, length + 1 : length + 2].astype(I32), (positions, LANE))

    pairs = wanted.reshape(positions // GROUP, 1, GROUP, 1)
    twice = jnp.concatenate([pairs, pairs], axis=1).reshape(2 * positions, 1)
    place = lax.broadcasted_iota(I32, (2 * positions, 1), 0)
    moved = place // GROUP % 2 + place % GROUP
    every = lax.broadcasted_iota(I32, (2 * positions, TURNS * rows), 1)
    for q in range(2):
        picks = every == (2 * q + moved) % TURNS * rows + twice
        frames[q] = jnp.dot(
            picks.astype(F32).astype(BF16), shifted[...], preferred_element_type=F32
        ).astype(BF16)
    either = lax.broadcasted_iota(I32, (positions, 2 * rows), 1)
    picks = (either == wanted) | (either == wanted + rows)
    picks = picks.astype(F32).astype(BF16)
    waves[:, width - LANE :] = jnp.where(
        lax.broadcasted_iota(I32, (positions, LANE), 1) < length - (width - LANE),
        waves[:, width - LANE :],
        0.0,
    )
    shape = (blocks * GROUP, LANE)
    member = lax.broadcasted_iota(I32, shape, 0) % GROUP
    low_half = member < TURNS
    turn = (lax.broadcasted_iota(I32, shape, 1) // STEP + 2 * TURNS - member) % TURNS

    for g in range(positions // GROUP):
        first = g * GROUP
        copies = toeplitz.at[g % toeplitz.shape[0]]
        for j in range(GROUP):
            wave = jnp.broadcast_to(waves[first + j : first + j + 1, :], (STEP, width))
            copies[j * STEP : (j + 1) * STEP, :] = pltpu.roll(
                wave, 0, axis=1, stride=1, stride_axis=0
            ).astype(BF16)
        at = slice(g * 2 * GROUP, (g + 1) * 2 * GROUP)
        data = [
            frames[q, at, a * LANE : a * LANE + width] for q in range(2) for a in range(blocks)
        ]
        product = lax.dot_general(
            jnp.concatenate(data, axis=0),
            copies[...],
            (((1,), (1,)), ((), ())),
            preferred_element_type=F32,
        )
        if g == 0:
            traces[...] = jnp.dot(picks, scales[...], preferred_element_type=F32)
        product = product.reshape(2, blocks, 2, GROUP, 2 * LANE)
        own = jnp.zeros(shape, F32)
        for step in range(TURNS):
            part = product[step // 2, :, step % 2].reshape(blocks * GROUP, 2 * LANE)
            part = jnp.where(low_half, part[:, :LANE], part[:, LANE:])
            if step > 0:
                part = pltpu.roll(part, step * STEP, axis=1)
            own = jnp.where(turn == step, part, own)
        own = own.reshape(blocks, GROUP, LANE)
        for a in range(blocks):
            at_lag = slice(a * LANE, (a + 1) * LANE)
            traces[first : first + GROUP, at_lag] = traces[first : first + GROUP, at_lag] * own[a]
        if (g + 1) % CHUNK == 0:
            for t in range(len(order)):
                total = jnp.zeros((GROUP, lags), F32) if g + 1 == CHUNK else sums[t]
                for done in range(g + 1 - CHUNK, g + 1):
                    ready = slice(done * GROUP, (done + 1) * GROUP)
                    mine = (template[ready] == t).astype(F32)
                    total = total + traces[ready, :] * jnp.concatenate([mine] * blocks, axis=1)
                if g + 1 < positions // GROUP:
                    sums[t] = total
                else:
                    tiles = [total[:, a * LANE : (a + 1) * LANE] for a in range(blocks)]
                    stacked[order.index(t)] = add_rows(tiles)


def per_device(window, prior, waves, chan_list, chan_count, station_row):
    sta_size = lax.axis_size("sta")
    sta_pos = lax.axis_index("sta").astype(I32).reshape(1)
    group_size, slot_count, length = waves.shape
    positions = group_size * slot_count
    block_rows = prior.shape[0]
    width = up(length + STEP, LANE)
    tpl_size = lax.axis_size("tpl")
    lags = window.shape[1] * tpl_size
    order = stacks_order(sta_size)
    vmem = pl.BlockSpec(memory_space=pltpu.VMEM)
    smem = pl.BlockSpec(memory_space=pltpu.SMEM)

    anywhere = pl.BlockSpec(memory_space=pl.ANY)
    sent = pl.pallas_call(
        functools.partial(route_kernel, sta_size, block_rows),
        out_shape=jax.ShapeDtypeStruct((positions, width), BF16),
        in_specs=[smem] + [anywhere] * 4,
        out_specs=vmem,
        scratch_shapes=[
            pltpu.VMEM((positions, length), BF16),
            pltpu.VMEM((group_size, slot_count), I32),
            pltpu.SMEM((group_size,), I32),
            pltpu.VMEM((1, station_row.shape[0]), I32),
            pltpu.VMEM((group_size, LANE), I32),
            pltpu.VMEM((positions, width), F32),
            pltpu.SemaphoreType.DMA((4,)),
        ],
        name="route",
    )(
        sta_pos,
        waves.reshape(positions, length),
        chan_list,
        chan_count,
        station_row.reshape(1, station_row.shape[0]),
    )
    arrived = lax.all_to_all(
        sent.reshape(sta_size, positions // sta_size, width),
        "sta",
        split_axis=0,
        concat_axis=0,
        tiled=True,
        axis_index_groups=[waves_order(sta_size)],
    ).reshape(positions, width)

    pieces, turns = [window], [0]
    distance = tpl_size // 2
    while distance >= 1:
        hop = distance | 1
        pairs = [(i, i ^ hop) for i in range(tpl_size)]
        pieces = pieces + [lax.ppermute(piece, "tpl", pairs) for piece in pieces]
        turns = turns + [turn ^ hop for turn in turns]
        distance //= 2
    total = up(prior.shape[1] + lags, LANE)
    used = lags - LANE + width
    shifted, scales = pl.pallas_call(
        functools.partial(prepare_kernel, length, turns),
        out_shape=[
            jax.ShapeDtypeStruct((TURNS * block_rows, used), BF16),
            jax.ShapeDtypeStruct((2 * block_rows, lags), BF16),
        ],
        in_specs=[smem] + [vmem] * (1 + tpl_size),
        out_specs=[vmem, vmem],
        scratch_shapes=[pltpu.VMEM((block_rows, total), F32)],
        compiler_params=pltpu.CompilerParams(vmem_limit_bytes=16 * MIB),
        name="prepare",
    )(lax.axis_index("tpl").astype(I32).reshape(1), prior, *pieces)

    each = group_size // sta_size
    templates = [o * each + i for o in order for i in range(each)]
    stacked = pl.pallas_call(
        functools.partial(correlate_kernel, length, templates),
        out_shape=jax.ShapeDtypeStruct((group_size, lags // LANE, LANE), F32),
        in_specs=[vmem] * 3,
        out_specs=vmem,
        scratch_shapes=[
            pltpu.VMEM((2, 2 * positions, used), BF16),
            pltpu.VMEM((positions, width), F32),
            pltpu.VMEM((positions, lags), F32),
            pltpu.VMEM((positions // GROUP, GROUP * STEP, width), BF16),
            pltpu.VMEM((group_size, GROUP, lags), F32),
        ],
        compiler_params=pltpu.CompilerParams(vmem_limit_bytes=16 * MIB),
        name="correlate",
    )(arrived, shifted, scales)
    parts = lax.all_to_all(
        stacked, "sta", split_axis=0, concat_axis=0, tiled=True, axis_index_groups=[order]
    )
    parts = parts.reshape(sta_size, each, lags // LANE, LANE)
    return jnp.sum(parts, axis=0).reshape(each, lags)


def solution(mesh):
    in_specs = (
        P("sta", "tpl"),
        P("sta", None),
        P("tpl", "sta", None),
        P("tpl", "sta"),
        P("tpl"),
        P(),
    )
    out_specs = P(("tpl", "sta"), None)
    return jax.shard_map(
        per_device, mesh=mesh, in_specs=in_specs, out_specs=out_specs, check_vma=False
    )
```

```python
import functools

import jax
import jax.numpy as jnp
from jax import lax
from jax.experimental import pallas as pl
from jax.experimental.pallas import tpu as pltpu
from jax.sharding import PartitionSpec as P

epsilon = 1e-06
LANE = 128
STEP = 32
GROUP = 8
CHUNK = 1
TURNS = LANE // STEP
MIB = 1 << 20
PARTS = 4
F32, BF16, I32 = jnp.float32, jnp.bfloat16, jnp.int32


def up(value, unit):
    return -(-value // unit) * unit


def column_sum(values):
    return jnp.sum(values, axis=1, keepdims=True)


def waves_order(size):
    if size == 8:
        return [3, 0, 1, 4, 5, 7, 2, 6]
    return [(i + size // 2 - 1) % size for i in range(size)]


def stacks_order(size):
    middle = size // 2
    order = []
    for odd in range(2):
        order += range(middle + odd, -1, -2)
        order += range(middle + odd + 2, size, 2)
    return order


def route_kernel(
    sta_size,
    block_rows,
    sta_pos,
    waves_in,
    chan_list_in,
    chan_count_in,
    station_row_in,
    sent,
    waves,
    chan_list,
    chan_count,
    station_row,
    channels,
    padded,
    arrivals,
):
    quarter = waves.shape[0] // PARTS
    parts = [pl.ds(i * quarter, quarter) for i in range(PARTS)]
    copies = [
        pltpu.make_async_copy(source, target, arrivals.at[i])
        for i, (source, target) in enumerate(
            (
                (chan_list_in, chan_list),
                (station_row_in, station_row),
                (chan_count_in, chan_count),
                *((waves_in.at[part], waves.at[part]) for part in parts),
            )
        )
    ]
    for copy in copies:
        copy.start()
    positions, length = waves.shape
    group_size, slot_count = chan_list.shape
    width = sent.shape[1]
    capacity = positions // sta_size
    padded[:, width - LANE :] = jnp.zeros((positions, LANE), F32)
    channels[...] = jnp.zeros(channels.shape, I32)
    row = lax.broadcasted_iota(I32, (positions, positions), 0)
    lane = lax.broadcasted_iota(I32, (positions, positions), 1)
    before = (row < lane).astype(F32).astype(BF16)
    spot = lax.broadcasted_iota(I32, (positions, 1), 0)
    slot = sta_pos[0] * slot_count + spot % slot_count
    along = lax.broadcasted_iota(I32, (1, positions), 1)
    for copy in copies[:3]:
        copy.wait()

    channels[:, :slot_count] = chan_list[...]
    channel = channels[...]
    station = (channel * 21846) >> 16
    found = jnp.zeros(channel.shape, I32)
    for first in range(0, station_row.shape[1], LANE):
        some = jnp.broadcast_to(station_row[:, first : first + LANE], channel.shape)
        place = jnp.clip(station - first, 0, LANE - 1)
        here = (station >= first) & (station < first + LANE)
        found = jnp.where(here, jnp.take_along_axis(some, place, axis=1), found)
    data_row = 3 * found + channel - 3 * station
    spread = jnp.where(lax.broadcasted_iota(I32, channel.shape, 1) < slot_count, data_row, 0)
    spread = pltpu.roll(spread.astype(F32), 0, axis=1, stride=slot_count, stride_axis=0)
    data_row = jnp.sum(spread, axis=0, keepdims=True).astype(I32)
    owner = jnp.zeros((1, positions), I32)
    for o in range(1, sta_size):
        owner = owner + (data_row >= o * block_rows).astype(I32)
    local_row = data_row - owner * block_rows
    hits = (lax.broadcasted_iota(I32, (sta_size, positions), 0) == owner).astype(F32)
    ahead = jnp.dot(hits.astype(BF16), before, preferred_element_type=F32)
    rank = jnp.sum(ahead * hits, axis=0, keepdims=True).astype(I32)
    place = jnp.zeros((1, positions), I32)
    for k, o in enumerate(waves_order(sta_size)):
        place = jnp.where(owner == o, k * capacity, place)
    goes = row == place + rank
    row_tag = column_sum(jnp.where(goes, local_row, 0).astype(F32))
    template_tag = column_sum(jnp.where(goes, along // slot_count, 0).astype(F32))

    count = jnp.zeros((positions, 1), I32)
    for t in range(group_size):
        count = jnp.where(spot // slot_count == t, chan_count[t], count)
    for copy in copies[3:]:
        copy.wait()
    padded[:, :length] = waves[...].astype(F32)
    raw = padded[...]
    listed = (slot < count).astype(F32)
    gain = listed / jnp.sqrt(column_sum(raw * raw) + epsilon)
    ordered = jnp.dot(
        goes.astype(F32).astype(BF16), (raw * gain).astype(BF16), preferred_element_type=F32
    )
    wide = lax.broadcasted_iota(I32, (positions, width), 1)
    sent[...] = jnp.where(
        wide == length, row_tag, jnp.where(wide == length + 1, template_tag, ordered)
    ).astype(BF16)


def prepare_kernel(length, turns, tpl_pos, prior, *refs):
    pieces, (shifted, scales, extended) = refs[: len(turns)], refs[len(turns) :]
    rows, before = prior.shape
    piece = pieces[0].shape[1]
    lags = piece * len(turns)
    total = extended.shape[1]
    start = before // LANE * LANE
    extended[:, :start] = jnp.zeros((rows, start), F32)
    extended[:, start:] = jnp.zeros((rows, total - start), F32)
    for turn, part in zip(turns, pieces):
        first = pl.multiple_of(start + (tpl_pos[0] ^ turn) * piece, LANE)
        extended[:, pl.ds(first, piece)] = part[...].astype(F32)
    moved = pltpu.roll(extended[:, start:], before - start, axis=1)
    extended[:, start:] = jnp.zeros((rows, total - start), F32)
    extended[:, :before] = prior[...].astype(F32)
    extended[:, start:] = extended[:, start:] + moved
    whole = extended[...]
    used = shifted.shape[1]
    for turn in range(TURNS):
        moved = whole if turn == 0 else pltpu.roll(whole, total - turn * STEP, axis=1)
        shifted[turn * rows : (turn + 1) * rows, :] = moved[:, :used].astype(BF16)
    square = whole * whole
    high = square.astype(BF16)
    low = (square - high.astype(F32)).astype(BF16)
    over = length % LANE
    sample = lax.broadcasted_iota(I32, (2 * LANE, LANE), 0) % LANE
    lag = lax.broadcasted_iota(I32, (2 * LANE, LANE), 1)
    masks = [sample >= lag, sample < (lag + over) % LANE, sample >= 0]
    masks = jnp.concatenate([mask.astype(F32) for mask in masks], axis=1).astype(BF16)
    spans = [slice(k * LANE, (k + 1) * LANE) for k in range(total // LANE)]
    squares = [jnp.concatenate([high[:, at], low[:, at]], axis=1) for at in spans]
    sums = jnp.dot(jnp.concatenate(squares, axis=0), masks, preferred_element_type=F32)
    sums = sums.reshape(len(spans), rows, 3 * LANE)
    first, last, every = (sums[:, :, at] for at in spans[:3])
    inside = lax.broadcasted_iota(I32, (rows, LANE), 1) < LANE - over
    for a in range(lags // LANE):
        energy = first[a]
        for k in range(a + 1, a + length // LANE):
            energy = energy + every[k]
        end = a + length // LANE
        energy = energy + jnp.where(inside, last[end], every[end] + last[end + 1])
        scale = 1.0 / jnp.sqrt(energy + epsilon)
        scale_high = scale.astype(BF16)
        scales[:rows, spans[a]] = scale_high
        scales[rows:, spans[a]] = (scale - scale_high.astype(F32)).astype(BF16)


def add_rows(tiles):
    size = len(tiles)
    row = lax.broadcasted_iota(I32, tiles[0].shape, 0)
    step = size // 2
    while step >= 1:
        tiles = [
            jnp.where(
                row & step == 0,
                low + pltpu.roll(low, size - step, axis=0),
                high + pltpu.roll(high, step, axis=0),
            )
            for low, high in zip(tiles[:step], tiles[step:])
        ]
        step //= 2
    return tiles[0]


def correlate_kernel(
    length, order, arrived, shifted, scales, stacked, frames, waves, traces, toeplitz, sums
):
    positions, width = arrived.shape
    rows = scales.shape[0] // 2
    lags = scales.shape[1]
    blocks = lags // LANE
    waves[...] = arrived[...].astype(F32)
    wanted = waves[:, length : length + 1].astype(I32)
    template = jnp.broadcast_to(waves[:, length + 1 : length + 2].astype(I32), (positions, LANE))

    pairs = wanted.reshape(positions // GROUP, 1, GROUP, 1)
    twice = jnp.concatenate([pairs, pairs], axis=1).reshape(2 * positions, 1)
    place = lax.broadcasted_iota(I32, (2 * positions, 1), 0)
    moved = place // GROUP % 2 + place % GROUP
    every = lax.broadcasted_iota(I32, (2 * positions, TURNS * rows), 1)
    for q in range(2):
        picks = every == (2 * q + moved) % TURNS * rows + twice
        frames[q] = jnp.dot(
            picks.astype(F32).astype(BF16), shifted[...], preferred_element_type=F32
        ).astype(BF16)
    either = lax.broadcasted_iota(I32, (positions, 2 * rows), 1)
    picks = (either == wanted) | (either == wanted + rows)
    picks = picks.astype(F32).astype(BF16)
    waves[:, width - LANE :] = jnp.where(
        lax.broadcasted_iota(I32, (positions, LANE), 1) < length - (width - LANE),
        waves[:, width - LANE :],
        0.0,
    )
    shape = (blocks * GROUP, LANE)
    member = lax.broadcasted_iota(I32, shape, 0) % GROUP
    low_half = member < TURNS
    turn = (lax.broadcasted_iota(I32, shape, 1) // STEP + 2 * TURNS - member) % TURNS

    for g in range(positions // GROUP):
        first = g * GROUP
        copies = toeplitz.at[g % toeplitz.shape[0]]
        for j in range(GROUP):
            wave = jnp.broadcast_to(waves[first + j : first + j + 1, :], (STEP, width))
            copies[j * STEP : (j + 1) * STEP, :] = pltpu.roll(
                wave, 0, axis=1, stride=1, stride_axis=0
            ).astype(BF16)
        at = slice(g * 2 * GROUP, (g + 1) * 2 * GROUP)
        data = [
            frames[q, at, a * LANE : a * LANE + width] for q in range(2) for a in range(blocks)
        ]
        product = lax.dot_general(
            jnp.concatenate(data, axis=0),
            copies[...],
            (((1,), (1,)), ((), ())),
            preferred_element_type=F32,
        )
        if g == 0:
            traces[...] = jnp.dot(picks, scales[...], preferred_element_type=F32)
        product = product.reshape(2, blocks, 2, GROUP, 2 * LANE)
        own = jnp.zeros(shape, F32)
        for step in range(TURNS):
            part = product[step // 2, :, step % 2].reshape(blocks * GROUP, 2 * LANE)
            part = jnp.where(low_half, part[:, :LANE], part[:, LANE:])
            if step > 0:
                part = pltpu.roll(part, step * STEP, axis=1)
            own = jnp.where(turn == step, part, own)
        own = own.reshape(blocks, GROUP, LANE)
        for a in range(blocks):
            at_lag = slice(a * LANE, (a + 1) * LANE)
            traces[first : first + GROUP, at_lag] = traces[first : first + GROUP, at_lag] * own[a]
        if (g + 1) % CHUNK == 0:
            for t in range(len(order)):
                total = jnp.zeros((GROUP, lags), F32) if g + 1 == CHUNK else sums[t]
                for done in range(g + 1 - CHUNK, g + 1):
                    ready = slice(done * GROUP, (done + 1) * GROUP)
                    mine = (template[ready] == t).astype(F32)
                    total = total + traces[ready, :] * jnp.concatenate([mine] * blocks, axis=1)
                if g + 1 < positions // GROUP:
                    sums[t] = total
                else:
                    tiles = [total[:, a * LANE : (a + 1) * LANE] for a in range(blocks)]
                    stacked[order.index(t)] = add_rows(tiles)


def per_device(window, prior, waves, chan_list, chan_count, station_row):
    sta_size = lax.axis_size("sta")
    sta_pos = lax.axis_index("sta").astype(I32).reshape(1)
    group_size, slot_count, length = waves.shape
    positions = group_size * slot_count
    block_rows = prior.shape[0]
    width = up(length + STEP, LANE)
    tpl_size = lax.axis_size("tpl")
    lags = window.shape[1] * tpl_size
    order = stacks_order(sta_size)
    vmem = pl.BlockSpec(memory_space=pltpu.VMEM)
    smem = pl.BlockSpec(memory_space=pltpu.SMEM)

    anywhere = pl.BlockSpec(memory_space=pl.ANY)
    sent = pl.pallas_call(
        functools.partial(route_kernel, sta_size, block_rows),
        out_shape=jax.ShapeDtypeStruct((positions, width), BF16),
        in_specs=[smem] + [anywhere] * 4,
        out_specs=vmem,
        scratch_shapes=[
            pltpu.VMEM((positions, length), BF16),
            pltpu.VMEM((group_size, slot_count), I32),
            pltpu.SMEM((group_size,), I32),
            pltpu.VMEM((1, station_row.shape[0]), I32),
            pltpu.VMEM((group_size, LANE), I32),
            pltpu.VMEM((positions, width), F32),
            pltpu.SemaphoreType.DMA((3 + PARTS,)),
        ],
        name="route",
    )(
        sta_pos,
        waves.reshape(positions, length),
        chan_list,
        chan_count,
        station_row.reshape(1, station_row.shape[0]),
    )
    arrived = lax.all_to_all(
        sent.reshape(sta_size, positions // sta_size, width),
        "sta",
        split_axis=0,
        concat_axis=0,
        tiled=True,
        axis_index_groups=[waves_order(sta_size)],
    ).reshape(positions, width)

    pieces, turns = [window], [0]
    distance = tpl_size // 2
    while distance >= 1:
        hop = distance | 1
        pairs = [(i, i ^ hop) for i in range(tpl_size)]
        pieces = pieces + [lax.ppermute(piece, "tpl", pairs) for piece in pieces]
        turns = turns + [turn ^ hop for turn in turns]
        distance //= 2
    total = up(prior.shape[1] + lags, LANE)
    used = lags - LANE + width
    shifted, scales = pl.pallas_call(
        functools.partial(prepare_kernel, length, turns),
        out_shape=[
            jax.ShapeDtypeStruct((TURNS * block_rows, used), BF16),
            jax.ShapeDtypeStruct((2 * block_rows, lags), BF16),
        ],
        in_specs=[smem] + [vmem] * (1 + tpl_size),
        out_specs=[vmem, vmem],
        scratch_shapes=[pltpu.VMEM((block_rows, total), F32)],
        compiler_params=pltpu.CompilerParams(vmem_limit_bytes=16 * MIB),
        name="prepare",
    )(lax.axis_index("tpl").astype(I32).reshape(1), prior, *pieces)

    each = group_size // sta_size
    templates = [o * each + i for o in order for i in range(each)]
    stacked = pl.pallas_call(
        functools.partial(correlate_kernel, length, templates),
        out_shape=jax.ShapeDtypeStruct((group_size, lags // LANE, LANE), F32),
        in_specs=[vmem] * 3,
        out_specs=vmem,
        scratch_shapes=[
            pltpu.VMEM((2, 2 * positions, used), BF16),
            pltpu.VMEM((positions, width), F32),
            pltpu.VMEM((positions, lags), F32),
            pltpu.VMEM((positions // GROUP, GROUP * STEP, width), BF16),
            pltpu.VMEM((group_size, GROUP, lags), F32),
        ],
        compiler_params=pltpu.CompilerParams(vmem_limit_bytes=16 * MIB),
        name="correlate",
    )(arrived, shifted, scales)
    parts = lax.all_to_all(
        stacked, "sta", split_axis=0, concat_axis=0, tiled=True, axis_index_groups=[order]
    )
    parts = parts.reshape(sta_size, each, lags // LANE, LANE)
    return jnp.sum(parts, axis=0).reshape(each, lags)


def solution(mesh):
    in_specs = (
        P("sta", "tpl"),
        P("sta", None),
        P("tpl", "sta", None),
        P("tpl", "sta"),
        P("tpl"),
        P(),
    )
    out_specs = P(("tpl", "sta"), None)
    return jax.shard_map(
        per_device, mesh=mesh, in_specs=in_specs, out_specs=out_specs, check_vma=False
    )
```

```python
import functools

import jax
import jax.numpy as jnp
from jax import lax
from jax.experimental import pallas as pl
from jax.experimental.pallas import tpu as pltpu
from jax.sharding import PartitionSpec as P

epsilon = 1e-06
LANE = 128
STEP = 32
GROUP = 8
CHUNK = 1
TURNS = LANE // STEP
MIB = 1 << 20
F32, BF16, I32 = jnp.float32, jnp.bfloat16, jnp.int32


def up(value, unit):
    return -(-value // unit) * unit


def column_sum(values):
    return jnp.sum(values, axis=1, keepdims=True)


def waves_order(size):
    if size == 8:
        return [3, 0, 1, 5, 4, 7, 2, 6]
    return [(i + size // 2 - 1) % size for i in range(size)]


def stacks_order(size):
    middle = size // 2
    order = []
    for odd in range(2):
        order += range(middle + odd, -1, -2)
        order += range(middle + odd + 2, size, 2)
    return order


def route_kernel(
    sta_size,
    block_rows,
    sta_pos,
    waves_in,
    chan_list_in,
    chan_count_in,
    station_row_in,
    sent,
    waves,
    chan_list,
    chan_count,
    station_row,
    channels,
    padded,
    arrivals,
):
    copies = [
        pltpu.make_async_copy(source, target, arrivals.at[i])
        for i, (source, target) in enumerate(
            (
                (chan_list_in, chan_list),
                (station_row_in, station_row),
                (chan_count_in, chan_count),
                (waves_in, waves),
            )
        )
    ]
    for copy in copies:
        copy.start()
    positions, length = waves.shape
    group_size, slot_count = chan_list.shape
    width = sent.shape[1]
    capacity = positions // sta_size
    padded[:, width - LANE :] = jnp.zeros((positions, LANE), F32)
    channels[...] = jnp.zeros(channels.shape, I32)
    row = lax.broadcasted_iota(I32, (positions, positions), 0)
    lane = lax.broadcasted_iota(I32, (positions, positions), 1)
    before = (row < lane).astype(F32).astype(BF16)
    spot = lax.broadcasted_iota(I32, (positions, 1), 0)
    slot = sta_pos[0] * slot_count + spot % slot_count
    along = lax.broadcasted_iota(I32, (1, positions), 1)
    for copy in copies[:3]:
        copy.wait()

    channels[:, :slot_count] = chan_list[...]
    channel = channels[...]
    station = (channel * 21846) >> 16
    found = jnp.zeros(channel.shape, I32)
    for first in range(0, station_row.shape[1], LANE):
        some = jnp.broadcast_to(station_row[:, first : first + LANE], channel.shape)
        place = jnp.clip(station - first, 0, LANE - 1)
        here = (station >= first) & (station < first + LANE)
        found = jnp.where(here, jnp.take_along_axis(some, place, axis=1), found)
    data_row = 3 * found + channel - 3 * station
    spread = jnp.where(lax.broadcasted_iota(I32, channel.shape, 1) < slot_count, data_row, 0)
    spread = pltpu.roll(spread.astype(F32), 0, axis=1, stride=slot_count, stride_axis=0)
    data_row = jnp.sum(spread, axis=0, keepdims=True).astype(I32)
    owner = jnp.zeros((1, positions), I32)
    for o in range(1, sta_size):
        owner = owner + (data_row >= o * block_rows).astype(I32)
    local_row = data_row - owner * block_rows
    hits = (lax.broadcasted_iota(I32, (sta_size, positions), 0) == owner).astype(F32)
    ahead = jnp.dot(hits.astype(BF16), before, preferred_element_type=F32)
    rank = jnp.sum(ahead * hits, axis=0, keepdims=True).astype(I32)
    place = jnp.zeros((1, positions), I32)
    for k, o in enumerate(waves_order(sta_size)):
        place = jnp.where(owner == o, k * capacity, place)
    goes = row == place + rank
    row_tag = column_sum(jnp.where(goes, local_row, 0).astype(F32))
    template_tag = column_sum(jnp.where(goes, along // slot_count, 0).astype(F32))

    count = jnp.zeros((positions, 1), I32)
    for t in range(group_size):
        count = jnp.where(spot // slot_count == t, chan_count[t], count)
    copies[3].wait()
    padded[:, :length] = waves[...].astype(F32)
    raw = padded[...]
    listed = (slot < count).astype(F32)
    gain = listed / jnp.sqrt(column_sum(raw * raw) + epsilon)
    ordered = jnp.dot(
        goes.astype(F32).astype(BF16), (raw * gain).astype(BF16), preferred_element_type=F32
    )
    wide = lax.broadcasted_iota(I32, (positions, width), 1)
    sent[...] = jnp.where(
        wide == length, row_tag, jnp.where(wide == length + 1, template_tag, ordered)
    ).astype(BF16)


def prepare_kernel(length, turns, tpl_pos, prior, *refs):
    pieces, (shifted, scales, extended) = refs[: len(turns)], refs[len(turns) :]
    rows, before = prior.shape
    piece = pieces[0].shape[1]
    lags = piece * len(turns)
    total = extended.shape[1]
    start = before // LANE * LANE
    extended[:, :start] = jnp.zeros((rows, start), F32)
    extended[:, start:] = jnp.zeros((rows, total - start), F32)
    for turn, part in zip(turns, pieces):
        first = pl.multiple_of(start + (tpl_pos[0] ^ turn) * piece, LANE)
        extended[:, pl.ds(first, piece)] = part[...].astype(F32)
    moved = pltpu.roll(extended[:, start:], before - start, axis=1)
    extended[:, start:] = jnp.zeros((rows, total - start), F32)
    extended[:, :before] = prior[...].astype(F32)
    extended[:, start:] = extended[:, start:] + moved
    whole = extended[...]
    used = shifted.shape[1]
    for turn in range(TURNS):
        moved = whole if turn == 0 else pltpu.roll(whole, total - turn * STEP, axis=1)
        shifted[turn * rows : (turn + 1) * rows, :] = moved[:, :used].astype(BF16)
    square = whole * whole
    high = square.astype(BF16)
    low = (square - high.astype(F32)).astype(BF16)
    over = length % LANE
    sample = lax.broadcasted_iota(I32, (2 * LANE, LANE), 0) % LANE
    lag = lax.broadcasted_iota(I32, (2 * LANE, LANE), 1)
    masks = [sample >= lag, sample < (lag + over) % LANE, sample >= 0]
    masks = jnp.concatenate([mask.astype(F32) for mask in masks], axis=1).astype(BF16)
    spans = [slice(k * LANE, (k + 1) * LANE) for k in range(total // LANE)]
    squares = [jnp.concatenate([high[:, at], low[:, at]], axis=1) for at in spans]
    sums = jnp.dot(jnp.concatenate(squares, axis=0), masks, preferred_element_type=F32)
    sums = sums.reshape(len(spans), rows, 3 * LANE)
    first, last, every = (sums[:, :, at] for at in spans[:3])
    inside = lax.broadcasted_iota(I32, (rows, LANE), 1) < LANE - over
    for a in range(lags // LANE):
        energy = first[a]
        for k in range(a + 1, a + length // LANE):
            energy = energy + every[k]
        end = a + length // LANE
        energy = energy + jnp.where(inside, last[end], every[end] + last[end + 1])
        scale = 1.0 / jnp.sqrt(energy + epsilon)
        scale_high = scale.astype(BF16)
        scales[:rows, spans[a]] = scale_high
        scales[rows:, spans[a]] = (scale - scale_high.astype(F32)).astype(BF16)


def add_rows(tiles):
    size = len(tiles)
    row = lax.broadcasted_iota(I32, tiles[0].shape, 0)
    step = size // 2
    while step >= 1:
        tiles = [
            jnp.where(
                row & step == 0,
                low + pltpu.roll(low, size - step, axis=0),
                high + pltpu.roll(high, step, axis=0),
            )
            for low, high in zip(tiles[:step], tiles[step:])
        ]
        step //= 2
    return tiles[0]


def correlate_kernel(
    length, order, arrived, shifted, scales, stacked, frames, waves, traces, toeplitz, sums
):
    positions, width = arrived.shape
    rows = scales.shape[0] // 2
    lags = scales.shape[1]
    blocks = lags // LANE
    waves[...] = arrived[...].astype(F32)
    wanted = waves[:, length : length + 1].astype(I32)
    template = jnp.broadcast_to(waves[:, length + 1 : length + 2].astype(I32), (positions, LANE))

    pairs = wanted.reshape(positions // GROUP, 1, GROUP, 1)
    twice = jnp.concatenate([pairs, pairs], axis=1).reshape(2 * positions, 1)
    place = lax.broadcasted_iota(I32, (2 * positions, 1), 0)
    moved = place // GROUP % 2 + place % GROUP
    every = lax.broadcasted_iota(I32, (2 * positions, TURNS * rows), 1)
    for q in range(2):
        picks = every == (2 * q + moved) % TURNS * rows + twice
        frames[q] = jnp.dot(
            picks.astype(F32).astype(BF16), shifted[...], preferred_element_type=F32
        ).astype(BF16)
    either = lax.broadcasted_iota(I32, (positions, 2 * rows), 1)
    picks = (either == wanted) | (either == wanted + rows)
    picks = picks.astype(F32).astype(BF16)
    waves[:, width - LANE :] = jnp.where(
        lax.broadcasted_iota(I32, (positions, LANE), 1) < length - (width - LANE),
        waves[:, width - LANE :],
        0.0,
    )
    shape = (blocks * GROUP, LANE)
    member = lax.broadcasted_iota(I32, shape, 0) % GROUP
    low_half = member < TURNS
    turn = (lax.broadcasted_iota(I32, shape, 1) // STEP + 2 * TURNS - member) % TURNS

    for g in range(positions // GROUP):
        first = g * GROUP
        copies = toeplitz.at[g % toeplitz.shape[0]]
        for j in range(GROUP):
            wave = jnp.broadcast_to(waves[first + j : first + j + 1, :], (STEP, width))
            copies[j * STEP : (j + 1) * STEP, :] = pltpu.roll(
                wave, 0, axis=1, stride=1, stride_axis=0
            ).astype(BF16)
        at = slice(g * 2 * GROUP, (g + 1) * 2 * GROUP)
        data = [
            frames[q, at, a * LANE : a * LANE + width] for q in range(2) for a in range(blocks)
        ]
        product = lax.dot_general(
            jnp.concatenate(data, axis=0),
            copies[...],
            (((1,), (1,)), ((), ())),
            preferred_element_type=F32,
        )
        if g == 0:
            traces[...] = jnp.dot(picks, scales[...], preferred_element_type=F32)
        product = product.reshape(2, blocks, 2, GROUP, 2 * LANE)
        own = jnp.zeros(shape, F32)
        for step in range(TURNS):
            part = product[step // 2, :, step % 2].reshape(blocks * GROUP, 2 * LANE)
            part = jnp.where(low_half, part[:, :LANE], part[:, LANE:])
            if step > 0:
                part = pltpu.roll(part, step * STEP, axis=1)
            own = jnp.where(turn == step, part, own)
        own = own.reshape(blocks, GROUP, LANE)
        for a in range(blocks):
            at_lag = slice(a * LANE, (a + 1) * LANE)
            traces[first : first + GROUP, at_lag] = traces[first : first + GROUP, at_lag] * own[a]
        if (g + 1) % CHUNK == 0:
            for t in range(len(order)):
                total = jnp.zeros((GROUP, lags), F32) if g + 1 == CHUNK else sums[t]
                for done in range(g + 1 - CHUNK, g + 1):
                    ready = slice(done * GROUP, (done + 1) * GROUP)
                    mine = (template[ready] == t).astype(F32)
                    total = total + traces[ready, :] * jnp.concatenate([mine] * blocks, axis=1)
                if g + 1 < positions // GROUP:
                    sums[t] = total
                else:
                    tiles = [total[:, a * LANE : (a + 1) * LANE] for a in range(blocks)]
                    stacked[order.index(t)] = add_rows(tiles)


def per_device(window, prior, waves, chan_list, chan_count, station_row):
    sta_size = lax.axis_size("sta")
    sta_pos = lax.axis_index("sta").astype(I32).reshape(1)
    group_size, slot_count, length = waves.shape
    positions = group_size * slot_count
    block_rows = prior.shape[0]
    width = up(length + STEP, LANE)
    tpl_size = lax.axis_size("tpl")
    lags = window.shape[1] * tpl_size
    order = stacks_order(sta_size)
    vmem = pl.BlockSpec(memory_space=pltpu.VMEM)
    smem = pl.BlockSpec(memory_space=pltpu.SMEM)

    anywhere = pl.BlockSpec(memory_space=pl.ANY)
    sent = pl.pallas_call(
        functools.partial(route_kernel, sta_size, block_rows),
        out_shape=jax.ShapeDtypeStruct((positions, width), BF16),
        in_specs=[smem] + [anywhere] * 4,
        out_specs=vmem,
        scratch_shapes=[
            pltpu.VMEM((positions, length), BF16),
            pltpu.VMEM((group_size, slot_count), I32),
            pltpu.SMEM((group_size,), I32),
            pltpu.VMEM((1, station_row.shape[0]), I32),
            pltpu.VMEM((group_size, LANE), I32),
            pltpu.VMEM((positions, width), F32),
            pltpu.SemaphoreType.DMA((4,)),
        ],
        name="route",
    )(
        sta_pos,
        waves.reshape(positions, length),
        chan_list,
        chan_count,
        station_row.reshape(1, station_row.shape[0]),
    )
    arrived = lax.all_to_all(
        sent.reshape(sta_size, positions // sta_size, width),
        "sta",
        split_axis=0,
        concat_axis=0,
        tiled=True,
        axis_index_groups=[waves_order(sta_size)],
    ).reshape(positions, width)

    pieces, turns = [window], [0]
    distance = tpl_size // 2
    while distance >= 1:
        hop = distance | 1
        pairs = [(i, i ^ hop) for i in range(tpl_size)]
        pieces = pieces + [lax.ppermute(piece, "tpl", pairs) for piece in pieces]
        turns = turns + [turn ^ hop for turn in turns]
        distance //= 2
    total = up(prior.shape[1] + lags, LANE)
    used = lags - LANE + width
    shifted, scales = pl.pallas_call(
        functools.partial(prepare_kernel, length, turns),
        out_shape=[
            jax.ShapeDtypeStruct((TURNS * block_rows, used), BF16),
            jax.ShapeDtypeStruct((2 * block_rows, lags), BF16),
        ],
        in_specs=[smem] + [vmem] * (1 + tpl_size),
        out_specs=[vmem, vmem],
        scratch_shapes=[pltpu.VMEM((block_rows, total), F32)],
        compiler_params=pltpu.CompilerParams(vmem_limit_bytes=16 * MIB),
        name="prepare",
    )(lax.axis_index("tpl").astype(I32).reshape(1), prior, *pieces)

    each = group_size // sta_size
    templates = [o * each + i for o in order for i in range(each)]
    stacked = pl.pallas_call(
        functools.partial(correlate_kernel, length, templates),
        out_shape=jax.ShapeDtypeStruct((group_size, lags // LANE, LANE), F32),
        in_specs=[vmem] * 3,
        out_specs=vmem,
        scratch_shapes=[
            pltpu.VMEM((2, 2 * positions, used), BF16),
            pltpu.VMEM((positions, width), F32),
            pltpu.VMEM((positions, lags), F32),
            pltpu.VMEM((positions // GROUP, GROUP * STEP, width), BF16),
            pltpu.VMEM((group_size, GROUP, lags), F32),
        ],
        compiler_params=pltpu.CompilerParams(vmem_limit_bytes=16 * MIB),
        name="correlate",
    )(arrived, shifted, scales)
    parts = lax.all_to_all(
        stacked, "sta", split_axis=0, concat_axis=0, tiled=True, axis_index_groups=[order]
    )
    parts = parts.reshape(sta_size, each, lags // LANE, LANE)
    return jnp.sum(parts, axis=0).reshape(each, lags)


def solution(mesh):
    in_specs = (
        P("sta", "tpl"),
        P("sta", None),
        P("tpl", "sta", None),
        P("tpl", "sta"),
        P("tpl"),
        P(),
    )
    out_specs = P(("tpl", "sta"), None)
    return jax.shard_map(
        per_device, mesh=mesh, in_specs=in_specs, out_specs=out_specs, check_vma=False
    )
```
